256 devices in a mesh: ctx: 64 (over z, x, core), head: 4 (over y).
Axes of the slice: x: 4, y: 4, z: 8, core: 2. Of those that a mesh axis runs over, the one named last changes fastest.
Arguments:
- queries: bfloat16 [4096, 128, 576], P('ctx', 'head'), may hold values from -40 to 40
- latent: bfloat16 [131072, 576], P('ctx'), may hold values from -8 to 8
- index_queries: bfloat16 [4096, 64, 128], P('ctx', 'head'), may hold values from -6 to 6
- index_weights: bfloat16 [4096, 64], P('ctx', 'head'), may hold values from -0.75 to 0.75
- index_keys: bfloat16 [131072, 128], P('ctx'), may hold values from -6 to 6
- request_tiles: int32 [64, 64, 2], P('ctx'), may hold values from 0 to 15, as said below
- selection: int32 [4096, 16], P('ctx'), may hold values from 0 to 127, as said below
Outputs:
- attended: bfloat16 [4096, 128, 512], P('ctx', 'head')
- index_scores: float32 [4096, 2048], P('ctx', 'head')
The draws below stay inside these ranges and needn't reach their ends.
Inputs may be any that keep to these rules, and one draw needn't show every extreme that they name: `request_tiles`: entry [r, o, c] is a tile number local to owner o, all different for one r and o. Live slots are a leading run of each owner's slots; all 2 slots of an owner are live unless the owner holds fewer than 2 tiles at or before the tile of device r's last query. `selection`: row q lists 16 different live request slots of device q // 64. Their tiles lie at or before the tile holding position 126976 + q, and that tile is one of them.
All inputs are finite; a program needn't handle non-finite values.
Results may differ from the reference program's by a relative error of at most 0.007.
Values may be sent and summed in bfloat16 or wider, within the bound.
No kernel may reach another device: no remote copies, remote signals or barrier semaphores. Data moves between devices by JAX's collectives and lax.ppermute only.
A program may use at most 128 MiB of HBM per device.

```python
import jax
import jax.numpy as jnp
from jax import lax

KEY_VALUE_RANK = 512
LATENT = 576
HEADS = 128
IHEADS = 64
IDIM = 128
TILE = 128
K_TILES = 16
TOPK = 2048
TOK_DEV = 2048
Q_DEV = 64
CACHED_POSITIONS = 131072
QUERIES = 4096
CAP = 2
N_CTX = 64


def request_plan(key):
    base_key = jax.random.fold_in(key, 11)
    key_force = jax.random.fold_in(base_key, 0)
    key_tile = jax.random.fold_in(base_key, 2)
    key_pick = jax.random.fold_in(base_key, 3)
    key_order = jax.random.fold_in(base_key, 4)
    tile_count = TOK_DEV // TILE
    slot_total = N_CTX * CAP
    forced = jax.random.randint(key_force, (), 0, (CACHED_POSITIONS - QUERIES) // TOK_DEV)
    requester = jnp.arange(N_CTX, dtype=jnp.int32)
    diagonal_entries = (CACHED_POSITIONS - QUERIES + requester * Q_DEV) // TILE
    owners = jnp.arange(N_CTX, dtype=jnp.int32)
    local_ids = jnp.arange(tile_count, dtype=jnp.int32)
    global_tile = owners[:, None] * tile_count + local_ids[None, :]
    earlier = global_tile[None] < diagonal_entries[:, None, None]
    own_tile = global_tile[None] == diagonal_entries[:, None, None]
    noise = jax.random.randint(key_tile, (N_CTX, N_CTX, tile_count), 0, 65536)
    ranking = (noise + 65536 * earlier.astype(jnp.int32) + 131072 * own_tile.astype(jnp.int32)) * tile_count + local_ids
    tiles = lax.top_k(ranking, CAP)[1].astype(jnp.int32)
    usable = jnp.sum((earlier | own_tile).astype(jnp.int32), axis=2)
    counts = jnp.minimum(CAP, usable)
    slot_ids = jnp.arange(slot_total, dtype=jnp.int32)
    live_slots = slot_ids[None, :] % CAP < jnp.repeat(counts, CAP, axis=1)
    query_ids = jnp.arange(QUERIES, dtype=jnp.int32)
    device_of = query_ids // Q_DEV
    diag_slot = diagonal_entries // tile_count * CAP
    forced_slot = forced * CAP
    pick_noise = jax.random.randint(key_pick, (QUERIES, slot_total), 0, 65536)
    pinned = (slot_ids[None, :] == diag_slot[device_of][:, None]) | (slot_ids[None, :] == forced_slot)
    pinned = pinned | (device_of[:, None] == N_CTX - 1) & (slot_ids[None, :] == slot_total - 1)
    pinned = pinned | (device_of[:, None] == 0) & (slot_ids[None, :] == 0)
    boost = live_slots[device_of].astype(jnp.int32) * 65536 + pinned.astype(jnp.int32) * 131072
    chosen = lax.top_k((pick_noise + boost) * slot_total + slot_ids[None, :], K_TILES)[1].astype(jnp.int32)
    order_keys = jax.random.randint(key_order, (QUERIES, K_TILES), 0, 65536) * K_TILES + jnp.arange(K_TILES, dtype=jnp.int32)[None, :]
    order = jnp.argsort(order_keys, axis=1)
    selection = jnp.take_along_axis(chosen, order, axis=1)
    return (forced, tiles, selection)


def latent_rows(latent_key, tile_ids, adjust):

    def tile_rows(tile_index):
        values_raw = jnp.clip(jax.random.normal(jax.random.fold_in(latent_key, tile_index), (TILE, LATENT), jnp.float32), -5.5, 5.5)
        spread = jax.random.uniform(jax.random.fold_in(latent_key, tile_index + CACHED_POSITIONS), (TILE, 1), jnp.float32, 0.6, 1.4)
        values_raw = values_raw * (1.0 + adjust * (spread - 1.0))
        values_raw = values_raw.at[0].set(values_raw[0])
        values_raw = values_raw.at[1].set(values_raw[1])
        return values_raw
    return jax.vmap(tile_rows)(tile_ids)


def draw_request_tiles(key, part):
    plan = request_plan(key)
    return plan[1]


def draw_selection(key, part):
    plan = request_plan(key)
    return plan[2]


def draw_latent(key, part):
    key = jax.random.fold_in(key, 21)
    tile_ids = jnp.arange(CACHED_POSITIONS // TILE, dtype=jnp.int32)
    values = latent_rows(key, tile_ids, 0.0)
    return values.reshape(CACHED_POSITIONS, LATENT).astype(jnp.bfloat16)


def draw_queries(key, part):
    key = jax.random.fold_in(key, 31)
    return jnp.clip(jax.random.normal(key, (QUERIES, HEADS, LATENT), jnp.float32), -6.0, 6.0).astype(jnp.bfloat16)


def block_levels(rng, extent, cuts, smallest, top_value):
    loudness, own = 1.0, jax.random.fold_in(rng, 6)
    for axis_at, blocks in cuts:
        draws = jnp.exp(jax.random.uniform(jax.random.fold_in(own, axis_at), (blocks,), jnp.float32, smallest / len(cuts), top_value / len(cuts)))
        loudness = loudness * jnp.repeat(draws, extent[axis_at] // blocks).reshape([-1 if axis == axis_at else 1 for axis in range(len(extent))])
    return loudness


def normal_values(stream_key, extent, scale, most, cuts=(), held_as=jnp.bfloat16):
    result = scale * jax.random.normal(stream_key, extent, jnp.float32)
    if cuts:
        result = result * block_levels(stream_key, extent, cuts, -0.22, 0.18)
    return jnp.clip(result, -most, most).astype(held_as)


def setup_inputs(seed: int = 0) -> dict:
    streams_of = jax.random.split(jax.random.key(seed), 8)
    return {
        "queries": draw_queries(jax.random.fold_in(streams_of[7], 71), 0),
        "latent": draw_latent(jax.random.fold_in(streams_of[7], 71), 0),
        "index_queries": normal_values(streams_of[2], (QUERIES, IHEADS, IDIM), 1.0, 6.0, ((0, 64), (1, 4))),
        "index_weights": normal_values(streams_of[3], (QUERIES, IHEADS), 0.125, 0.75, ((0, 64), (1, 4))),
        "index_keys": normal_values(streams_of[4], (CACHED_POSITIONS, IDIM), 1.0, 6.0, ((0, 64),)),
        "request_tiles": draw_request_tiles(jax.random.fold_in(streams_of[7], 71), 0),
        "selection": draw_selection(jax.random.fold_in(streams_of[7], 71), 0),
    }


score_scale = 192.0 ** -0.5


def reference(queries, latent, index_queries, index_weights, index_keys, request_tiles, selection):
    tile_count = TOK_DEV // TILE
    query_ids = jnp.arange(QUERIES, dtype=jnp.int32)
    owner_ids = (selection // CAP).astype(jnp.int32)
    local_tile = request_tiles[(query_ids // Q_DEV)[:, None], owner_ids, selection % CAP]
    global_tile = owner_ids * tile_count + local_tile
    key_pos = (global_tile[:, :, None] * TILE + jnp.arange(TILE, dtype=jnp.int32)[None, None, :]).reshape(QUERIES, TOPK)
    query_pos = CACHED_POSITIONS - QUERIES + query_ids
    visible = key_pos <= query_pos[:, None]

    def attend(pieces):
        query_block, index_query_block, iw_block, pos_block, vis_block = pieces
        gathered = latent[pos_block].astype(jnp.float32)
        collected_keys = index_keys[pos_block].astype(jnp.float32)
        scores = jnp.einsum("bhl,bkl->bhk", query_block.astype(jnp.float32), gathered) * score_scale
        scores = jnp.where(vis_block[:, None, :], scores, -1e30)
        row_peak = jnp.max(scores, axis=2, keepdims=True)
        weights = jnp.exp(scores - row_peak)
        probabilities = lax.optimization_barrier((weights / jnp.sum(weights, axis=2, keepdims=True)).astype(jnp.bfloat16))
        attended = jnp.einsum("bhk,bkv->bhv", probabilities.astype(jnp.float32), gathered[:, :, :KEY_VALUE_RANK]).astype(jnp.bfloat16)
        key_products = jnp.einsum("urc,ulc->url", index_query_block.astype(jnp.float32), collected_keys)
        relu_dots = jnp.maximum(key_products, 0.0) * (IDIM ** -0.5)
        summed_total = jnp.einsum("bg,bgk->bk", iw_block.astype(jnp.float32), relu_dots)
        return attended, jnp.where(vis_block, summed_total, 0.0)

    blocks = QUERIES // Q_DEV
    shaped = (queries.reshape(blocks, Q_DEV, HEADS, LATENT),
              index_queries.reshape(blocks, Q_DEV, IHEADS, IDIM),
              index_weights.reshape(blocks, Q_DEV, IHEADS),
              key_pos.reshape(blocks, Q_DEV, TOPK),
              visible.reshape(blocks, Q_DEV, TOPK))
    attended, index_scores = lax.map(attend, shaped)
    return attended.reshape(QUERIES, HEADS, KEY_VALUE_RANK), index_scores.reshape(QUERIES, TOPK)
```

```python
import functools

import jax
import jax.numpy as jnp
from jax import lax
from jax.experimental import pallas as pl
from jax.experimental.pallas import tpu as pltpu
from jax.sharding import Mesh, PartitionSpec as P

KEY_VALUE_RANK = 512
LATENT = 576
INDEX_AT = 640
WIDTH = 768
TILE = 128
CAP = 2
GROUP = 8
SCALE = 192.0 ** -0.5
LOG2_E = 1.4426950408889634
MASKED = -1e30


def attend_kernel(sel, q, iq, weight_t, lim, *refs):
    fetched, (out, lse, index_out, rows, picked_a, picked_b, sems) = refs[:-7], refs[-7:]
    step = pl.program_id(0)
    part = rows.shape[0] // (sel.shape[1] * 8)
    picks = sel.shape[1]
    heads = q.shape[0] * q.shape[2]
    index_heads = iq.shape[0] * iq.shape[2]

    @pl.when(step == 0)
    def _():
        copies, at = [], 0
        for i, ref in enumerate(fetched):
            size = ref.shape[0]
            copies.append(pltpu.make_async_copy(ref, rows.at[pl.ds(at, size)], sems.at[i]))
            at += size
        for copy in copies:
            copy.start()
        for copy in copies:
            copy.wait()

    lane = lax.broadcasted_iota(jnp.int32, (heads, 128), 1)
    weight_lane = lax.broadcasted_iota(jnp.int32, weight_t.shape, 1)
    lse_columns = jnp.zeros((heads, 128), jnp.float32)
    for i in range(GROUP):
        picked = (picked_a, picked_b)[i % 2]
        query = step * GROUP + i
        for k in range(picks):
            start = pl.multiple_of(sel[query, k] * part, part)
            picked[pl.ds(k * part, part), :] = rows[pl.ds(start, part), :]
        visible = lim[pl.ds(i, 1), :] >= 0
        scores = lax.dot_general(
            q[:, i].reshape(heads, LATENT),
            picked[:, :LATENT],
            (((1,), (1,)), ((), ())),
            preferred_element_type=jnp.float32,
        )
        scores = jnp.where(visible, scores * (SCALE * LOG2_E), MASKED)
        peak = jnp.max(scores, axis=1, keepdims=True)
        probs = jnp.exp2(scores - peak)
        total = jnp.sum(probs, axis=1, keepdims=True)
        summed = jnp.dot(
            probs.astype(jnp.bfloat16), picked[:, :KEY_VALUE_RANK], preferred_element_type=jnp.float32
        )
        summed = (summed * (1.0 / total)).astype(jnp.bfloat16)
        out[:, i] = summed.reshape(q.shape[0], q.shape[2], KEY_VALUE_RANK)
        lse_columns = jnp.where(lane == i, peak + jnp.log2(total), lse_columns)
        dots = lax.dot_general(
            iq[:, i].reshape(index_heads, iq.shape[3]),
            picked[:, INDEX_AT:],
            (((1,), (1,)), ((), ())),
            preferred_element_type=jnp.float32,
        )
        weight = jnp.sum(jnp.where(weight_lane == query, weight_t[...], 0.0), axis=1, keepdims=True)
        index_row = jnp.sum(jnp.maximum(dots, 0.0) * weight, axis=0, keepdims=True)
        index_out[pl.ds(i, 1), :] = jnp.where(visible, index_row, 0.0)
    lse[...] = jnp.transpose(lse_columns)[:GROUP]


def attend(sel, q, iq, weight_t, lim, fetched):
    ways, queries, heads, width = q.shape
    picks = sel.shape[1]
    part = lim.shape[1] // picks
    slots = sum(f.shape[0] for f in fetched) // part
    grid = queries // GROUP
    spec = pltpu.PrefetchScalarGridSpec(
        num_scalar_prefetch=1,
        grid=(grid,),
        in_specs=[
            pl.BlockSpec((ways, GROUP, heads, width), lambda i, s: (0, i, 0, 0)),
            pl.BlockSpec((ways, GROUP) + iq.shape[2:], lambda i, s: (0, i, 0, 0)),
            pl.BlockSpec(weight_t.shape, lambda i, s: (0, 0)),
            pl.BlockSpec((GROUP, lim.shape[1]), lambda i, s: (i, 0)),
        ]
        + [pl.BlockSpec(memory_space=pl.ANY)] * len(fetched),
        out_specs=[
            pl.BlockSpec((ways, GROUP, heads, KEY_VALUE_RANK), lambda i, s: (0, i, 0, 0)),
            pl.BlockSpec((GROUP, ways * heads), lambda i, s: (i, 0)),
            pl.BlockSpec((GROUP, lim.shape[1]), lambda i, s: (i, 0)),
        ],
        scratch_shapes=[
            pltpu.VMEM((slots * part, WIDTH), jnp.bfloat16),
            pltpu.VMEM((picks * part, WIDTH), jnp.bfloat16),
            pltpu.VMEM((picks * part, WIDTH), jnp.bfloat16),
            pltpu.SemaphoreType.DMA((len(fetched),)),
        ],
    )
    return pl.pallas_call(
        attend_kernel,
        grid_spec=spec,
        out_shape=[
            jax.ShapeDtypeStruct((ways, queries, heads, KEY_VALUE_RANK), jnp.bfloat16),
            jax.ShapeDtypeStruct((queries, ways * heads), jnp.float32),
            jax.ShapeDtypeStruct((queries, lim.shape[1]), jnp.float32),
        ],
        compiler_params=pltpu.CompilerParams(vmem_limit_bytes=48 * 1024 * 1024),
        name="attend",
    )(sel, q, iq, weight_t, lim, *fetched)


def ring_blocks(block, axis, size):
    forward = [(i, (i + 1) % size) for i in range(size)]
    backward = [(i, (i - 1) % size) for i in range(size)]
    up = down = block
    got = {0: block}
    for d in range(1, size // 2):
        up = lax.ppermute(up, axis, forward)
        down = lax.ppermute(down, axis, backward)
        got[size - d], got[d] = up, down
    half = block.shape[0] // 2
    got[size // 2] = jnp.concatenate(
        [lax.ppermute(up[:half], axis, forward), lax.ppermute(down[half:], axis, backward)]
    )
    return got


def rounds_of(size):
    rounds = [[0, 1, size - 1]]
    rounds += [[d, size - d] for d in range(2, size // 2)]
    return rounds + [[size // 2]]


def shards(queries, latent, index_queries, index_weights, index_keys, request_tiles, selection):
    z_count, x_count, c_count, y_count = (lax.axis_size(a) for a in ("z", "x", "c", "y"))
    z, x, c, y = (lax.axis_index(a) for a in ("z", "x", "c", "y"))
    plane = x_count * c_count
    here = x * c_count + c
    query_count, local_heads, _ = queries.shape
    tile_count = latent.shape[0] // TILE
    part = TILE // y_count
    picks = selection.shape[1]

    own_rows = lax.dynamic_index_in_dim(latent.reshape(tile_count, y_count, part, LATENT), y, 1, False)
    own_keys = lax.dynamic_index_in_dim(index_keys.reshape(tile_count, y_count, part, -1), y, 1, False)
    padding = jnp.zeros((tile_count, part, INDEX_AT - LATENT), own_rows.dtype)
    own = jnp.concatenate([own_rows, padding, own_keys], axis=2)

    all_queries = lax.all_gather(queries, "y")
    all_index_queries = lax.all_gather(index_queries, "y")
    all_index_weights = lax.all_gather(index_weights, "y")

    wanted = request_tiles[0]
    plans = lax.all_gather(wanted, ("x", "c")).reshape(plane, z_count, plane, CAP)
    plans = lax.dynamic_index_in_dim(plans, here, 2, False)

    blocks = ring_blocks(own, "z", z_count)
    fetched = []
    place = {}
    base = 0
    for distances in rounds_of(z_count):
        found = []
        for p, d in enumerate(distances):
            asked = lax.dynamic_index_in_dim(plans, (z + d) % z_count, 1, False)
            found.append(blocks[d][asked])
            place[d] = (base + p * CAP, len(distances) * CAP)
        found = jnp.stack(found, axis=1).reshape(plane, -1, WIDTH)
        moved = lax.all_to_all(found, ("x", "c"), split_axis=0, concat_axis=0, tiled=True)
        fetched.append(moved.reshape(-1, WIDTH))
        base += plane * len(distances) * CAP

    owner = selection // CAP
    distance = (owner // plane - z) % z_count
    first = sum(jnp.where(distance == d, place[d][0], 0) for d in place)
    stride = sum(jnp.where(distance == d, place[d][1], 0) for d in place)
    rows_at = first + (owner % plane) * stride + selection % CAP

    flat_wanted = wanted.reshape(-1)
    matches = selection[:, :, None] == jnp.arange(flat_wanted.shape[0], dtype=jnp.int32)
    local_tile = jnp.sum(jnp.where(matches, flat_wanted, 0), axis=2)
    tile_start = (owner * tile_count + local_tile) * TILE + y * part
    ctx_count = z_count * plane
    context = ctx_count * tile_count * TILE
    query_pos = (
        context
        - ctx_count * query_count
        + (z * plane + here) * query_count
        + jnp.arange(query_count, dtype=jnp.int32)
    )
    lim = (query_pos[:, None] - tile_start)[:, :, None] - jnp.arange(part, dtype=jnp.int32)
    lim = lim.reshape(query_count, picks * part)

    key_scale = index_keys.shape[1] ** -0.5
    weight_t = jnp.transpose(all_index_weights.astype(jnp.float32), (0, 2, 1)).reshape(-1, query_count) * key_scale

    partial, lse, index_part = attend(rows_at, all_queries, all_index_queries, weight_t, lim, fetched)

    lse = jnp.transpose(lse.reshape(query_count, y_count, local_heads), (1, 0, 2))
    index_part = jnp.transpose(index_part.reshape(query_count, y_count, -1), (1, 0, 2))
    small = jnp.concatenate([lse, index_part], axis=2)
    small = lax.all_to_all(small, "y", split_axis=0, concat_axis=0, tiled=True)
    partial = lax.all_to_all(partial, "y", split_axis=0, concat_axis=0, tiled=True)
    lse, index_part = small[:, :, :local_heads], small[:, :, local_heads:]
    share = jnp.exp2(lse - jnp.max(lse, axis=0))
    share = share / jnp.sum(share, axis=0)
    attended = jnp.sum(partial.astype(jnp.float32) * share[..., None], axis=0).astype(jnp.bfloat16)
    index_scores = jnp.transpose(
        index_part.reshape(y_count, query_count, picks // y_count, part), (1, 2, 0, 3)
    ).reshape(query_count, -1)
    return attended, index_scores


def solution(mesh):
    ctx, head = mesh.devices.shape
    x_count, c_count = 4, 2
    grid = Mesh(
        mesh.devices.reshape(ctx // (x_count * c_count), x_count, c_count, head), ("z", "x", "c", "y")
    )
    ctx_axes = ("z", "x", "c")
    return jax.shard_map(
        shards,
        mesh=grid,
        in_specs=(
            P(ctx_axes, "y", None),
            P(ctx_axes, None),
            P(ctx_axes, "y", None),
            P(ctx_axes, "y"),
            P(ctx_axes, None),
            P(ctx_axes, None, None),
            P(ctx_axes, None),
        ),
        out_specs=(P(ctx_axes, "y", None), P(ctx_axes, "y")),
        check_vma=False,
    )
```

```python
import jax
import jax.numpy as jnp
from jax import lax
from jax.experimental import pallas as pl
from jax.experimental.pallas import tpu as pltpu
from jax.sharding import Mesh, PartitionSpec as P

KEY_VALUE_RANK = 512
LATENT = 576
ROTARY = LATENT - KEY_VALUE_RANK
LANES = 128
COLUMNS = KEY_VALUE_RANK // LANES
WIDE = KEY_VALUE_RANK + LANES
TILE = 128
CAP = 2
GROUP = 8
BATCH = 4
SCALE = 192.0 ** -0.5
LOG2_E = 1.4426950408889634
MASKED = -1e30


def lines_of(part):
    latent = COLUMNS * part
    return latent, latent + part // 2, latent + part // 2 + part


def attend_kernel(sel, lim, quarters, q_own, q_pair, *refs):
    own_fetched, pair_fetched = refs[: len(refs) // 2 - 3], refs[len(refs) // 2 - 3 : -6]
    out_own, out_pair, lse, rows, rotary, sems = refs[-6:]
    step = pl.program_id(0)
    slots, half, _ = rows.shape
    part = half // 2
    latent, packed, _ = lines_of(part)
    picks = sel.shape[1]
    heads = q_own.shape[1] + q_pair.shape[1]

    @pl.when(step == 0)
    def _():
        copies = []
        for side, fetched in enumerate((own_fetched, pair_fetched)):
            at = 0
            for ref in fetched:
                count = ref.shape[0]
                for j in range(COLUMNS):
                    copies.append(
                        pltpu.make_async_copy(
                            ref.at[:, pl.ds(j * part, part), :],
                            rows.at[pl.ds(at, count), pl.ds(side * part, part), pl.ds(j * LANES, LANES)],
                            sems.at[len(copies)],
                        )
                    )
                copies.append(
                    pltpu.make_async_copy(
                        ref.at[:, pl.ds(latent, packed - latent), :],
                        rotary.at[pl.ds(at, count), pl.ds(side * (part // 2), part // 2), :],
                        sems.at[len(copies)],
                    )
                )
                at += count
        for copy in copies:
            copy.start()
        for copy in copies:
            copy.wait()

        @pl.loop(0, slots)
        def _(slot):
            for side in range(2):
                pairs = rotary[slot, pl.ds(side * (part // 2), part // 2), :]
                turned = jnp.concatenate([pairs[:, ROTARY:], pairs[:, :ROTARY]], axis=1)
                rows[slot, pl.ds(side * part, part), pl.ds(KEY_VALUE_RANK, LANES)] = jnp.concatenate(
                    [pairs, turned], axis=0
                )

    row = lax.broadcasted_iota(jnp.int32, (half, heads), 0)
    place = jnp.where(row < part, row + quarters[0] * part, row - part + quarters[1] * part)
    per = 256 // half

    def keys(query, n, width):
        return jnp.concatenate([rows[sel[query, n * per + j], :, :width] for j in range(per)], axis=0)

    def scores_of(i):
        query = step * GROUP + i
        here = jnp.concatenate([q_own[i], q_pair[i]], axis=0)
        found = []
        for n in range(picks // per):
            block = lax.dot_general(
                keys(query, n, LATENT), here, (((1,), (1,)), ((), ())), preferred_element_type=jnp.float32
            )
            block = block * (SCALE * LOG2_E)
            found += [
                jnp.where(place <= lim[query, n * per + j], block[j * half : (j + 1) * half], MASKED)
                for j in range(per)
            ]
        return jnp.concatenate(found, axis=0)

    for first in range(0, GROUP, BATCH):
        batch = range(first, first + BATCH)
        scores = [scores_of(i) for i in batch]
        probs = []
        for i, s in zip(batch, scores):
            peak = jnp.max(s, axis=0, keepdims=True)
            p = jnp.exp2(s - peak)
            total = jnp.sum(p, axis=0, keepdims=True)
            probs.append((p * (1.0 / total)).astype(jnp.bfloat16))
            lse[pl.ds(i, 1), pl.ds(0, heads)] = peak + jnp.log2(total)
        for i, p in zip(batch, probs):
            summed = 0.0
            for n in range(picks // per):
                summed = summed + lax.dot_general(
                    p[n * 256 : (n + 1) * 256],
                    keys(step * GROUP + i, n, KEY_VALUE_RANK),
                    (((0,), (0,)), ((), ())),
                    preferred_element_type=jnp.float32,
                )
            summed = summed.astype(jnp.bfloat16)
            out_own[i] = summed[: heads // 2]
            out_pair[i] = summed[heads // 2 :]


def attend(sel, lim, quarters, q_own, q_pair, own_fetched, pair_fetched, first, count):
    _, heads, width = q_own.shape
    slots = sum(f.shape[0] for f in own_fetched)
    part = 2 * pair_fetched[0].shape[1] // (2 * COLUMNS + 1)
    at = first // GROUP
    spec = pltpu.PrefetchScalarGridSpec(
        num_scalar_prefetch=3,
        grid=(count // GROUP,),
        in_specs=[pl.BlockSpec((GROUP, heads, width), lambda i, *_: (at + i, 0, 0))] * 2
        + [pl.BlockSpec(memory_space=pl.ANY)] * (2 * len(own_fetched)),
        out_specs=[pl.BlockSpec((GROUP, heads, KEY_VALUE_RANK), lambda i, *_: (i, 0, 0))] * 2
        + [pl.BlockSpec((GROUP, LANES), lambda i, *_: (i, 0))],
        scratch_shapes=[
            pltpu.VMEM((slots, 2 * part, WIDE), jnp.bfloat16),
            pltpu.VMEM((slots, part, LANES), jnp.bfloat16),
            pltpu.SemaphoreType.DMA((2 * len(own_fetched) * (COLUMNS + 1),)),
        ],
    )
    return pl.pallas_call(
        attend_kernel,
        grid_spec=spec,
        out_shape=[jax.ShapeDtypeStruct((count, heads, KEY_VALUE_RANK), jnp.bfloat16)] * 2
        + [jax.ShapeDtypeStruct((count, LANES), jnp.float32)],
        compiler_params=pltpu.CompilerParams(vmem_limit_bytes=40 * 1024 * 1024),
        name="attend",
    )(sel[first : first + count], lim[first : first + count], quarters, q_own, q_pair, *own_fetched, *pair_fetched)


def index_kernel(sel, iq, weight_t, lim, *refs):
    fetched, (index_out, keys, sems) = refs[:-3], refs[-3:]
    step = pl.program_id(0)
    part = keys.shape[1]
    _, packed, lines = lines_of(part)
    picks = sel.shape[1]
    heads = iq.shape[0] * iq.shape[2]

    @pl.when(step == 0)
    def _():
        copies, at = [], 0
        for i, ref in enumerate(fetched):
            count = ref.shape[0]
            copies.append(
                pltpu.make_async_copy(
                    ref.at[:, pl.ds(packed, lines - packed), :], keys.at[pl.ds(at, count)], sems.at[i]
                )
            )
            at += count
        for copy in copies:
            copy.start()
        for copy in copies:
            copy.wait()

    weight_lane = lax.broadcasted_iota(jnp.int32, weight_t.shape, 1)
    for i in range(GROUP):
        query = step * GROUP + i
        picked = jnp.concatenate([keys[sel[query, k]] for k in range(picks)], axis=0)
        dots = lax.dot_general(
            iq[:, i].reshape(heads, iq.shape[3]),
            picked,
            (((1,), (1,)), ((), ())),
            preferred_element_type=jnp.float32,
        )
        weight = jnp.sum(jnp.where(weight_lane == query, weight_t[...], 0.0), axis=1, keepdims=True)
        index_row = jnp.sum(jnp.maximum(dots, 0.0) * weight, axis=0, keepdims=True)
        index_out[pl.ds(i, 1), :] = jnp.where(lim[pl.ds(i, 1), :] >= 0, index_row, 0.0)


def index(sel, iq, weight_t, lim, fetched):
    queries, picks = sel.shape
    part = lim.shape[1] // picks
    slots = sum(f.shape[0] for f in fetched)
    spec = pltpu.PrefetchScalarGridSpec(
        num_scalar_prefetch=1,
        grid=(queries // GROUP,),
        in_specs=[
            pl.BlockSpec((iq.shape[0], GROUP) + iq.shape[2:], lambda i, s: (0, i, 0, 0)),
            pl.BlockSpec(weight_t.shape, lambda i, s: (0, 0)),
            pl.BlockSpec((GROUP, lim.shape[1]), lambda i, s: (i, 0)),
        ]
        + [pl.BlockSpec(memory_space=pl.ANY)] * len(fetched),
        out_specs=pl.BlockSpec((GROUP, lim.shape[1]), lambda i, s: (i, 0)),
        scratch_shapes=[
            pltpu.VMEM((slots, part, LANES), jnp.bfloat16),
            pltpu.SemaphoreType.DMA((len(fetched),)),
        ],
    )
    return pl.pallas_call(
        index_kernel,
        grid_spec=spec,
        out_shape=jax.ShapeDtypeStruct(lim.shape, jnp.float32),
        compiler_params=pltpu.CompilerParams(vmem_limit_bytes=16 * 1024 * 1024),
        name="index",
    )(sel, iq, weight_t, lim, *fetched)


def ring_blocks(block, axis, size):
    forward = [(i, (i + 1) % size) for i in range(size)]
    backward = [(i, (i - 1) % size) for i in range(size)]
    up = down = block
    got = {0: block}
    for d in range(1, size // 2):
        up = lax.ppermute(up, axis, forward)
        down = lax.ppermute(down, axis, backward)
        got[size - d], got[d] = up, down
    half = block.shape[0] // 2
    got[size // 2] = jnp.concatenate(
        [lax.ppermute(up[:half], axis, forward), lax.ppermute(down[half:], axis, backward)]
    )
    return got


def rounds_of(size):
    rounds = [[0, 1, size - 1]]
    rounds += [[d, size - d] for d in range(2, size // 2)]
    return rounds + [[size // 2]]


def pairings():
    near, far = (lambda y: y ^ 1), (lambda y: 3 - y)
    rows = [(4 * c + y, 4 * c + (near, far)[c](y)) for c in range(2) for y in range(4)]
    heads = [(4 * c + y, 4 * c + (far, near)[c](y)) for c in range(2) for y in range(4)]
    return rows, heads


def shards(queries, latent, index_queries, index_weights, index_keys, request_tiles, selection):
    z_count, x_count, c_count, y_count = (lax.axis_size(a) for a in ("z", "x", "c", "y"))
    z, x, c, y = (lax.axis_index(a) for a in ("z", "x", "c", "y"))
    plane = x_count * c_count
    here = x * c_count + c
    query_count, local_heads, _ = queries.shape
    index_heads = index_queries.shape[1]
    tile_count = latent.shape[0] // TILE
    part = TILE // y_count
    picks = selection.shape[1]
    _, packed, lines = lines_of(part)
    row_pairs, head_pairs = pairings()

    def quarter(a):
        return lax.dynamic_index_in_dim(a.reshape(tile_count, y_count, part, a.shape[1]), y, 1, False)

    own_rows, own_keys = quarter(latent), quarter(index_keys)
    rotary = own_rows[:, :, KEY_VALUE_RANK:]
    own = jnp.concatenate(
        [own_rows[:, :, j * LANES : (j + 1) * LANES] for j in range(COLUMNS)]
        + [jnp.concatenate([rotary[:, : part // 2], rotary[:, part // 2 :]], axis=2), own_keys],
        axis=1,
    )

    q_pair = lax.ppermute(queries, ("c", "y"), head_pairs)
    weight_rows = jnp.pad(index_weights, ((0, 0), (0, LANES - index_heads)))
    joined = jnp.concatenate([index_queries, weight_rows.reshape(-1, index_heads, LANES)], axis=0)
    joined = lax.all_gather(joined, "y")
    weights = joined[:, query_count:].reshape(y_count, query_count, LANES)[:, :, :index_heads]
    key_scale = index_keys.shape[1] ** -0.5
    weight_t = jnp.transpose(weights.astype(jnp.float32), (0, 2, 1)).reshape(-1, query_count) * key_scale

    wanted = request_tiles[0]
    plans = lax.all_gather(wanted, ("x", "c")).reshape(plane, z_count, plane, CAP)
    plans = lax.dynamic_index_in_dim(plans, here, 2, False)

    blocks = ring_blocks(own, "z", z_count)
    own_fetched, pair_fetched = [], []
    place = {}
    base = 0
    for distances in rounds_of(z_count):
        found = []
        for p, d in enumerate(distances):
            asked = lax.dynamic_index_in_dim(plans, (z + d) % z_count, 1, False)
            found.append(blocks[d][asked])
            place[d] = (base + p * CAP, len(distances) * CAP)
        found = jnp.concatenate(found, axis=1).reshape(plane, -1, LANES)
        moved = lax.all_to_all(found, ("x", "c"), split_axis=0, concat_axis=0, tiled=True)
        moved = moved.reshape(-1, lines, LANES)
        own_fetched.append(moved)
        pair_fetched.append(lax.ppermute(moved[:, :packed], ("c", "y"), row_pairs))
        base += plane * len(distances) * CAP

    owner = selection // CAP
    distance = (owner // plane - z) % z_count
    first = sum(jnp.where(distance == d, place[d][0], 0) for d in place)
    stride = sum(jnp.where(distance == d, place[d][1], 0) for d in place)
    rows_at = first + (owner % plane) * stride + selection % CAP

    flat_wanted = wanted.reshape(-1)
    matches = selection[:, :, None] == jnp.arange(flat_wanted.shape[0], dtype=jnp.int32)
    local_tile = jnp.sum(jnp.where(matches, flat_wanted, 0), axis=2)
    tile_start = (owner * tile_count + local_tile) * TILE
    ctx_count = z_count * plane
    context = ctx_count * tile_count * TILE
    query_pos = (
        context
        - ctx_count * query_count
        + (z * plane + here) * query_count
        + jnp.arange(query_count, dtype=jnp.int32)
    )
    lim = query_pos[:, None] - tile_start
    own_lim = (lim - y * part)[:, :, None] - jnp.arange(part, dtype=jnp.int32)
    own_lim = own_lim.reshape(query_count, picks * part)
    partner = jnp.where(c == 0, y ^ 1, 3 - y)

    index_part = index(rows_at, joined, weight_t, own_lim, own_fetched)
    index_part = lax.all_gather(index_part, "y").reshape(y_count, query_count, y_count, -1, part)
    index_part = lax.dynamic_index_in_dim(index_part, y, 2, False)
    index_scores = jnp.transpose(index_part, (1, 2, 0, 3)).reshape(query_count, -1)

    quarters = jnp.stack([y, partner])
    attended = []
    split = query_count * 3 // 4
    for first_query, count in ((0, split), (split, query_count - split)):
        mine, other, lse = attend(
            rows_at, lim, quarters, queries, q_pair, own_fetched, pair_fetched, first_query, count
        )
        other = lax.ppermute(other, ("c", "y"), head_pairs)
        other_lse = lax.ppermute(lse[:, local_heads : 2 * local_heads], ("c", "y"), head_pairs)
        share = 1.0 / (1.0 + jnp.exp2(other_lse - lse[:, :local_heads]))[..., None]
        other_share = 1.0 / (1.0 + jnp.exp2(lse[:, :local_heads] - other_lse))[..., None]
        merged = mine.astype(jnp.float32) * share + other.astype(jnp.float32) * other_share
        attended.append(merged.astype(jnp.bfloat16))
    return jnp.concatenate(attended, axis=0), index_scores


def solution(mesh):
    ctx, head = mesh.devices.shape
    x_count, c_count = 4, 2
    grid = Mesh(
        mesh.devices.reshape(ctx // (x_count * c_count), x_count, c_count, head), ("z", "x", "c", "y")
    )
    ctx_axes = ("z", "x", "c")
    return jax.shard_map(
        shards,
        mesh=grid,
        in_specs=(
            P(ctx_axes, "y", None),
            P(ctx_axes, None),
            P(ctx_axes, "y", None),
            P(ctx_axes, "y"),
            P(ctx_axes, None),
            P(ctx_axes, None, None),
            P(ctx_axes, None),
        ),
        out_specs=(P(ctx_axes, "y", None), P(ctx_axes, "y")),
        check_vma=False,
    )
```

```python
import jax
import jax.numpy as jnp
from jax import lax
from jax.experimental import pallas as pl
from jax.experimental.pallas import tpu as pltpu
from jax.sharding import Mesh, PartitionSpec as P

KEY_VALUE_RANK = 512
LANES = 128
COLUMNS = KEY_VALUE_RANK // LANES
TILE = 128
CAP = 2
GROUP = 8
BATCH = 4
SCALE = 192.0 ** -0.5
LOG2_E = 1.4426950408889634
MASKED = -1e30


def lines_of(part):
    latent = COLUMNS * part
    return latent, latent + part // 2, latent + part // 2 + part


def attend_kernel(sel, lim, quarters, q_own, q_pair, *refs):
    own_fetched, pair_fetched = refs[: len(refs) // 2 - 3], refs[len(refs) // 2 - 3 : -6]
    out_own, out_pair, lse, own, pair, sems = refs[-6:]
    step = pl.program_id(0)
    part = 2 * own.shape[1] // (2 * COLUMNS + 3)
    low = part // 2
    picks = sel.shape[1]
    half_heads = q_own.shape[1]
    heads = 2 * half_heads

    @pl.when(step == 0)
    def _():
        copies = []
        for rows, fetched in ((own, own_fetched), (pair, pair_fetched)):
            at = 0
            for ref in fetched:
                copies.append(
                    pltpu.make_async_copy(ref, rows.at[pl.ds(at, ref.shape[0])], sems.at[len(copies)])
                )
                at += ref.shape[0]
        for copy in copies:
            copy.start()
        for copy in copies:
            copy.wait()

    row = lax.broadcasted_iota(jnp.int32, (low, 2 * heads), 0)
    lane = lax.broadcasted_iota(jnp.int32, (low, 2 * heads), 1)
    row = jnp.where(lane < heads, row, row + low)
    places = [row + quarters[side] * part for side in range(2)]
    sides = (own, pair)
    per = 256 // (2 * low)
    blocks = range(0, picks, per)

    def half_rows(ref, slot, upper):
        return jnp.concatenate(
            [ref[slot, pl.ds(j * part + upper * low, low), :] for j in range(COLUMNS)], axis=1
        )

    def scores_of(i):
        query = step * GROUP + i
        here = jnp.concatenate([q_own[i], q_pair[i]], axis=0)
        value, rotary = here[:, :KEY_VALUE_RANK], here[:, KEY_VALUE_RANK:]
        no_value, no_rotary = jnp.zeros_like(value), jnp.zeros_like(rotary)
        weights = jnp.concatenate(
            [
                jnp.concatenate([value, no_value, rotary, no_rotary], axis=1),
                jnp.concatenate([no_value, value, no_rotary, rotary], axis=1),
            ],
            axis=0,
        )
        found = []
        for n in blocks:
            lines = []
            for k in range(n, n + per):
                slot = sel[query, k]
                for ref in sides:
                    lines.append(
                        jnp.concatenate(
                            [
                                half_rows(ref, slot, 0),
                                half_rows(ref, slot, 1),
                                ref[slot, pl.ds(COLUMNS * part, low), :],
                            ],
                            axis=1,
                        )
                    )
            block = lax.dot_general(
                jnp.concatenate(lines, axis=0),
                weights,
                (((1,), (1,)), ((), ())),
                preferred_element_type=jnp.float32,
            )
            block = block * (SCALE * LOG2_E)
            for k in range(n, n + per):
                for side in range(2):
                    at = ((k - n) * 2 + side) * low
                    found.append(jnp.where(places[side] <= lim[query, k], block[at : at + low], MASKED))
        return jnp.concatenate(found, axis=0)

    def both(row, op):
        return op(row, jnp.concatenate([row[:, heads:], row[:, :heads]], axis=1))

    for first in range(0, GROUP, BATCH):
        batch = range(first, first + BATCH)
        scores = [scores_of(i) for i in batch]
        probs = []
        for i, s in zip(batch, scores):
            peak = both(jnp.max(s, axis=0, keepdims=True), jnp.maximum)
            p = jnp.exp2(s - peak)
            total = both(jnp.sum(p, axis=0, keepdims=True), jnp.add)
            lse[pl.ds(i, 1), :] = peak + jnp.log2(total)
            probs.append(jnp.transpose((p * (1.0 / total)).astype(jnp.bfloat16)))
        for i, p in zip(batch, probs):
            query = step * GROUP + i
            summed = 0.0
            for n in blocks:
                for upper in range(2):
                    values = jnp.concatenate(
                        [half_rows(ref, sel[query, k], upper) for k in range(n, n + per) for ref in sides], axis=0
                    )
                    summed = summed + jnp.dot(
                        p[upper * heads : (upper + 1) * heads, n * 2 * low : (n + per) * 2 * low],
                        values,
                        preferred_element_type=jnp.float32,
                    )
            summed = summed.astype(jnp.bfloat16)
            out_own[i] = summed[:half_heads]
            out_pair[i] = summed[half_heads:]


def attend(sel, lim, quarters, q_own, q_pair, own_fetched, pair_fetched, first, count):
    _, heads, width = q_own.shape
    slots = sum(f.shape[0] for f in own_fetched)
    lines = own_fetched[0].shape[1]
    at = first // GROUP
    spec = pltpu.PrefetchScalarGridSpec(
        num_scalar_prefetch=3,
        grid=(count // GROUP,),
        in_specs=[pl.BlockSpec((GROUP, heads, width), lambda i, *_: (at + i, 0, 0))] * 2
        + [pl.BlockSpec(memory_space=pl.ANY)] * (2 * len(own_fetched)),
        out_specs=[pl.BlockSpec((GROUP, heads, KEY_VALUE_RANK), lambda i, *_: (i, 0, 0))] * 2
        + [pl.BlockSpec((GROUP, LANES), lambda i, *_: (i, 0))],
        scratch_shapes=[
            pltpu.VMEM((slots, lines, LANES), jnp.bfloat16),
            pltpu.VMEM((slots, lines, LANES), jnp.bfloat16),
            pltpu.SemaphoreType.DMA((2 * len(own_fetched),)),
        ],
    )
    return pl.pallas_call(
        attend_kernel,
        grid_spec=spec,
        out_shape=[jax.ShapeDtypeStruct((count, heads, KEY_VALUE_RANK), jnp.bfloat16)] * 2
        + [jax.ShapeDtypeStruct((count, LANES), jnp.float32)],
        compiler_params=pltpu.CompilerParams(vmem_limit_bytes=40 * 1024 * 1024),
        cost_estimate=pl.CostEstimate(
            flops=count * 400_000_000, bytes_accessed=12_000_000, transcendentals=count * 65536
        ),
        name="attend",
    )(sel[first : first + count], lim[first : first + count], quarters, q_own, q_pair, *own_fetched, *pair_fetched)


def take_kernel(asked, *refs):
    blocks, found = refs[:-1], refs[-1]
    for to in range(found.shape[0]):
        for p, block in enumerate(blocks):
            for slot in range(CAP):
                found[to, p * CAP + slot] = block[asked[p, to, slot]]


def take(asked, blocks):
    count, plane, _ = asked.shape
    tile = blocks[0].shape[1:]
    return pl.pallas_call(
        take_kernel,
        in_specs=[pl.BlockSpec(memory_space=pltpu.SMEM)] + [pl.BlockSpec(memory_space=pltpu.VMEM)] * count,
        out_specs=pl.BlockSpec(memory_space=pltpu.VMEM),
        out_shape=jax.ShapeDtypeStruct((plane, count * CAP) + tile, blocks[0].dtype),
        compiler_params=pltpu.CompilerParams(vmem_limit_bytes=16 * 1024 * 1024),
        cost_estimate=pl.CostEstimate(flops=0, bytes_accessed=count * 1_500_000, transcendentals=0),
        name="take",
    )(asked, *blocks)


def index_kernel(sel, iq, weight_t, lim, *refs):
    fetched, (index_out, keys, sems) = refs[:-3], refs[-3:]
    step = pl.program_id(0)
    part = keys.shape[1]
    _, packed, lines = lines_of(part)
    picks = sel.shape[1]
    heads = iq.shape[0] * iq.shape[2]

    @pl.when(step == 0)
    def _():
        copies, at = [], 0
        for i, ref in enumerate(fetched):
            count = ref.shape[0]
            copies.append(
                pltpu.make_async_copy(
                    ref.at[:, pl.ds(packed, lines - packed), :], keys.at[pl.ds(at, count)], sems.at[i]
                )
            )
            at += count
        for copy in copies:
            copy.start()
        for copy in copies:
            copy.wait()

    weight_lane = lax.broadcasted_iota(jnp.int32, weight_t.shape, 1)
    for i in range(GROUP):
        query = step * GROUP + i
        picked = jnp.concatenate([keys[sel[query, k]] for k in range(picks)], axis=0)
        dots = lax.dot_general(
            iq[:, i].reshape(heads, iq.shape[3]),
            picked,
            (((1,), (1,)), ((), ())),
            preferred_element_type=jnp.float32,
        )
        weight = jnp.sum(jnp.where(weight_lane == query, weight_t[...], 0.0), axis=1, keepdims=True)
        index_row = jnp.sum(jnp.maximum(dots, 0.0) * weight, axis=0, keepdims=True)
        index_out[pl.ds(i, 1), :] = jnp.where(lim[pl.ds(i, 1), :] >= 0, index_row, 0.0)


def index(sel, iq, weight_t, lim, fetched):
    queries, picks = sel.shape
    part = lim.shape[1] // picks
    slots = sum(f.shape[0] for f in fetched)
    spec = pltpu.PrefetchScalarGridSpec(
        num_scalar_prefetch=1,
        grid=(queries // GROUP,),
        in_specs=[
            pl.BlockSpec((iq.shape[0], GROUP) + iq.shape[2:], lambda i, s: (0, i, 0, 0)),
            pl.BlockSpec(weight_t.shape, lambda i, s: (0, 0)),
            pl.BlockSpec((GROUP, lim.shape[1]), lambda i, s: (i, 0)),
        ]
        + [pl.BlockSpec(memory_space=pl.ANY)] * len(fetched),
        out_specs=pl.BlockSpec((GROUP, lim.shape[1]), lambda i, s: (i, 0)),
        scratch_shapes=[
            pltpu.VMEM((slots, part, LANES), jnp.bfloat16),
            pltpu.SemaphoreType.DMA((len(fetched),)),
        ],
    )
    return pl.pallas_call(
        index_kernel,
        grid_spec=spec,
        out_shape=jax.ShapeDtypeStruct(lim.shape, jnp.float32),
        compiler_params=pltpu.CompilerParams(vmem_limit_bytes=16 * 1024 * 1024),
        name="index",
    )(sel, iq, weight_t, lim, *fetched)


def ring_blocks(block, axis, size):
    forward = [(i, (i + 1) % size) for i in range(size)]
    backward = [(i, (i - 1) % size) for i in range(size)]
    up = down = block
    got = {0: block}
    for d in range(1, size // 2):
        up = lax.ppermute(up, axis, forward)
        down = lax.ppermute(down, axis, backward)
        got[size - d], got[d] = up, down
    half = block.shape[0] // 2
    got[size // 2] = jnp.concatenate(
        [lax.ppermute(up[:half], axis, forward), lax.ppermute(down[half:], axis, backward)]
    )
    return got


def rounds_of(size):
    return [[0]] + [[d, size - d] for d in range(1, size // 2)] + [[size // 2]]


def pairings():
    near, far = (lambda y: y ^ 1), (lambda y: 3 - y)
    rows = [(4 * c + y, 4 * c + (near, far)[c](y)) for c in range(2) for y in range(4)]
    heads = [(4 * c + y, 4 * c + (far, near)[c](y)) for c in range(2) for y in range(4)]
    return rows, heads


def shards(queries, latent, index_queries, index_weights, index_keys, request_tiles, selection):
    z_count, x_count, c_count, y_count = (lax.axis_size(a) for a in ("z", "x", "c", "y"))
    z, x, c, y = (lax.axis_index(a) for a in ("z", "x", "c", "y"))
    plane = x_count * c_count
    here = x * c_count + c
    query_count, local_heads, _ = queries.shape
    index_heads = index_queries.shape[1]
    tile_count = latent.shape[0] // TILE
    part = TILE // y_count
    picks = selection.shape[1]
    _, _, lines = lines_of(part)
    row_pairs, head_pairs = pairings()

    def quarter(a):
        return lax.dynamic_index_in_dim(a.reshape(tile_count, y_count, part, a.shape[1]), y, 1, False)

    own_rows, own_keys = quarter(latent), quarter(index_keys)
    rotary = own_rows[:, :, KEY_VALUE_RANK:]
    own = jnp.concatenate(
        [own_rows[:, :, j * LANES : (j + 1) * LANES] for j in range(COLUMNS)]
        + [jnp.concatenate([rotary[:, : part // 2], rotary[:, part // 2 :]], axis=2), own_keys],
        axis=1,
    )

    q_pair = lax.ppermute(queries, ("c", "y"), head_pairs)
    weight_rows = jnp.pad(index_weights, ((0, 0), (0, LANES - index_heads)))
    joined = jnp.concatenate([index_queries, weight_rows.reshape(-1, index_heads, LANES)], axis=0)
    joined = lax.all_gather(joined, "y")
    weights = joined[:, query_count:].reshape(y_count, query_count, LANES)[:, :, :index_heads]
    key_scale = index_keys.shape[1] ** -0.5
    weight_t = jnp.transpose(weights.astype(jnp.float32), (0, 2, 1)).reshape(-1, query_count) * key_scale

    wanted = request_tiles[0]
    plans = lax.all_gather(wanted, ("x", "c")).reshape(plane, z_count, plane, CAP)
    plans = lax.dynamic_index_in_dim(plans, here, 2, False)

    blocks = ring_blocks(own, "z", z_count)
    own_fetched, pair_fetched = [], []
    place = {}
    base = 0
    for r, distances in enumerate(rounds_of(z_count)):
        asked = jnp.stack(
            [lax.dynamic_index_in_dim(plans, (z + d) % z_count, 1, False) for d in distances]
        )
        found = take(asked, [blocks[d] for d in distances])
        for p, d in enumerate(distances):
            place[d] = (base + p * CAP, len(distances) * CAP)
        if r == 2:
            found, q_pair = lax.optimization_barrier((found, q_pair))
        if r >= 2:
            found, pair_fetched[r - 2] = lax.optimization_barrier((found, pair_fetched[r - 2]))
        moved = lax.all_to_all(found.reshape(plane, -1, LANES), ("x", "c"), split_axis=0, concat_axis=0, tiled=True)
        moved = moved.reshape(-1, lines, LANES)
        own_fetched.append(moved)
        pair_fetched.append(lax.ppermute(moved, ("c", "y"), row_pairs))
        base += plane * len(distances) * CAP

    owner = selection // CAP
    distance = (owner // plane - z) % z_count
    first = sum(jnp.where(distance == d, place[d][0], 0) for d in place)
    stride = sum(jnp.where(distance == d, place[d][1], 0) for d in place)
    rows_at = first + (owner % plane) * stride + selection % CAP

    flat_wanted = wanted.reshape(-1)
    matches = selection[:, :, None] == jnp.arange(flat_wanted.shape[0], dtype=jnp.int32)
    local_tile = jnp.sum(jnp.where(matches, flat_wanted, 0), axis=2)
    tile_start = (owner * tile_count + local_tile) * TILE
    ctx_count = z_count * plane
    context = ctx_count * tile_count * TILE
    query_pos = (
        context
        - ctx_count * query_count
        + (z * plane + here) * query_count
        + jnp.arange(query_count, dtype=jnp.int32)
    )
    lim = query_pos[:, None] - tile_start
    own_lim = (lim - y * part)[:, :, None] - jnp.arange(part, dtype=jnp.int32)
    own_lim = own_lim.reshape(query_count, picks * part)
    partner = jnp.where(c == 0, y ^ 1, 3 - y)

    index_part = index(rows_at, joined, weight_t, own_lim, own_fetched)
    rows_at, index_part = lax.optimization_barrier((rows_at, index_part))
    index_part = index_part.reshape(query_count, y_count, -1)
    from_quarter = []
    for d in range(y_count):
        piece = lax.dynamic_index_in_dim(index_part, (y + d) % y_count, 1, False)
        if d:
            piece = lax.ppermute(piece, "y", [(i, (i + d) % y_count) for i in range(y_count)])
        from_quarter.append(piece.reshape(query_count, -1, part))
    index_scores = jnp.concatenate(
        [
            sum(jnp.where((y - d) % y_count == j, from_quarter[d], 0.0) for d in range(y_count))[:, :, None]
            for j in range(y_count)
        ],
        axis=2,
    ).reshape(query_count, -1)

    quarters = jnp.stack([y, partner])
    attended = []
    split = query_count * 3 // 4
    for first_query, count in ((0, split), (split, query_count - split)):
        mine, other, lse = attend(
            rows_at, lim, quarters, queries, q_pair, own_fetched, pair_fetched, first_query, count
        )
        other = lax.ppermute(other, ("c", "y"), head_pairs)
        other_lse = lax.ppermute(lse[:, local_heads : 2 * local_heads], ("c", "y"), head_pairs)
        share = 1.0 / (1.0 + jnp.exp2(other_lse - lse[:, :local_heads]))[..., None]
        other_share = 1.0 / (1.0 + jnp.exp2(lse[:, :local_heads] - other_lse))[..., None]
        merged = mine.astype(jnp.float32) * share + other.astype(jnp.float32) * other_share
        attended.append(merged.astype(jnp.bfloat16))
    return jnp.concatenate(attended, axis=0), index_scores


def solution(mesh):
    ctx, head = mesh.devices.shape
    x_count, c_count = 4, 2
    grid = Mesh(
        mesh.devices.reshape(ctx // (x_count * c_count), x_count, c_count, head), ("z", "x", "c", "y")
    )
    ctx_axes = ("z", "x", "c")
    return jax.shard_map(
        shards,
        mesh=grid,
        in_specs=(
            P(ctx_axes, "y", None),
            P(ctx_axes, None),
            P(ctx_axes, "y", None),
            P(ctx_axes, "y"),
            P(ctx_axes, None),
            P(ctx_axes, None, None),
            P(ctx_axes, None),
        ),
        out_specs=(P(ctx_axes, "y", None), P(ctx_axes, "y")),
        check_vma=False,
    )
```

```python
import functools

import jax
import jax.numpy as jnp
from jax import lax
from jax.experimental import pallas as pl
from jax.experimental.pallas import tpu as pltpu
from jax.sharding import Mesh, PartitionSpec as P

KEY_VALUE_RANK = 512
LANES = 128
COLUMNS = KEY_VALUE_RANK // LANES
TILE = 128
CAP = 2
PART = 32
GROUP = 8
BATCH = 8
SCALE = 192.0 ** -0.5
LOG2_E = 1.4426950408889634
MASKED = -1e30


def lines_of(part):
    latent = COLUMNS * part
    return latent, latent + part // 2, latent + part // 2 + part


def attend_kernel(sel, lim, quarter, q_own, q_pair, *refs, merge, fetched_count):
    refs = list(refs)
    earlier, earlier_lse = (refs.pop(0), refs.pop(0)) if merge else (None, None)
    fetched, outs, (rows, sems) = refs[:fetched_count], refs[fetched_count:-2], refs[-2:]
    lse = outs[-1]
    step = pl.program_id(0)
    picks = sel.shape[1]
    half_heads = q_own.shape[1]
    heads = 2 * half_heads
    part = PART
    low = part // 2

    @pl.when(step == 0)
    def _():
        copies, at = [], 0
        for ref in fetched:
            size = ref.shape[0]
            copies.append(
                pltpu.make_async_copy(
                    ref.at[:, pl.ds(0, rows.shape[1])], rows.at[pl.ds(at, size)], sems.at[len(copies)]
                )
            )
            at += size
        for copy in copies:
            copy.start()
        for copy in copies:
            copy.wait()

    row = lax.broadcasted_iota(jnp.int32, (low, 2 * heads), 0)
    lane = lax.broadcasted_iota(jnp.int32, (low, 2 * heads), 1)
    place = jnp.where(lane < heads, row, row + low) + quarter[0] * part
    head = lax.broadcasted_iota(jnp.int32, (heads, 2 * heads), 0)
    own_lane = lax.broadcasted_iota(jnp.int32, (heads, 2 * heads), 1) == head

    def half_rows(slot, upper):
        return jnp.concatenate(
            [rows[slot, pl.ds(j * part + upper * low, low), :] for j in range(COLUMNS)], axis=1
        )

    def scores_of(i):
        query = step * GROUP + i
        here = jnp.concatenate([q_own[i], q_pair[i]], axis=0)
        value, rotary = here[:, :KEY_VALUE_RANK], here[:, KEY_VALUE_RANK:]
        no_value, no_rotary = jnp.zeros_like(value), jnp.zeros_like(rotary)
        weights = jnp.concatenate(
            [
                jnp.concatenate([value, no_value, rotary, no_rotary], axis=1),
                jnp.concatenate([no_value, value, no_rotary, rotary], axis=1),
            ],
            axis=0,
        )
        lines = []
        for k in range(picks):
            slot = sel[query, k]
            lines.append(
                jnp.concatenate(
                    [half_rows(slot, 0), half_rows(slot, 1), rows[slot, pl.ds(COLUMNS * part, low), :]], axis=1
                )
            )
        scores = lax.dot_general(
            jnp.concatenate(lines, axis=0),
            weights,
            (((1,), (1,)), ((), ())),
            preferred_element_type=jnp.float32,
        )
        scores = scores * (SCALE * LOG2_E)
        return jnp.concatenate(
            [
                jnp.where(place <= lim[query, k], scores[k * low : (k + 1) * low], MASKED)
                for k in range(picks)
            ],
            axis=0,
        )

    def both(row, op):
        return op(row, jnp.concatenate([row[:, heads:], row[:, :heads]], axis=1))

    for first in range(0, GROUP, BATCH):
        batch = range(first, first + BATCH)
        scores = [scores_of(i) for i in batch]
        probs, kept = [], []
        for i, s in zip(batch, scores):
            peak = both(jnp.max(s, axis=0, keepdims=True), jnp.maximum)
            p = jnp.exp2(s - peak)
            total = both(jnp.sum(p, axis=0, keepdims=True), jnp.add)
            level = peak + jnp.log2(total)
            if merge:
                before = earlier_lse[pl.ds(i, 1), :]
                top = jnp.maximum(before, level)
                old, new = jnp.exp2(before - top), jnp.exp2(level - top)
                share = 1.0 / (old + new)
                level = top + jnp.log2(old + new)
                kept.append(jnp.sum(jnp.where(own_lane, old * share, 0.0), axis=1, keepdims=True))
                p = p * (new * share / total)
            else:
                p = p * (1.0 / total)
            lse[pl.ds(i, 1), :] = level
            probs.append(jnp.transpose(p.astype(jnp.bfloat16)))
        for j, (i, p) in enumerate(zip(batch, probs)):
            query = step * GROUP + i
            summed = earlier[i].astype(jnp.float32) * kept[j] if merge else 0.0
            for upper in range(2):
                values = jnp.concatenate([half_rows(sel[query, k], upper) for k in range(picks)], axis=0)
                summed = summed + jnp.dot(
                    p[upper * heads : (upper + 1) * heads], values, preferred_element_type=jnp.float32
                )
            summed = summed.astype(jnp.bfloat16)
            if merge:
                outs[0][i] = summed[:half_heads]
                outs[1][i] = summed[half_heads:]
            else:
                outs[0][i] = summed


def attend(sel, lim, quarter, q_own, q_pair, fetched, first, count, earlier=None):
    _, heads, width = q_own.shape
    slots = sum(f.shape[0] for f in fetched)
    at = first // GROUP
    merge = earlier is not None
    lse_spec = pl.BlockSpec((GROUP, LANES), lambda i, *_: (i, 0))
    heads_out = [heads, heads] if merge else [2 * heads]
    before = [
        pl.BlockSpec((GROUP, 2 * heads, KEY_VALUE_RANK), lambda i, *_: (at + i, 0, 0)),
        pl.BlockSpec((GROUP, LANES), lambda i, *_: (at + i, 0)),
    ]
    spec = pltpu.PrefetchScalarGridSpec(
        num_scalar_prefetch=3,
        grid=(count // GROUP,),
        in_specs=[pl.BlockSpec((GROUP, heads, width), lambda i, *_: (at + i, 0, 0))] * 2
        + (before if merge else [])
        + [pl.BlockSpec(memory_space=pl.ANY)] * len(fetched),
        out_specs=[pl.BlockSpec((GROUP, n, KEY_VALUE_RANK), lambda i, *_: (i, 0, 0)) for n in heads_out]
        + [lse_spec],
        scratch_shapes=[
            pltpu.VMEM((slots, lines_of(PART)[1], LANES), jnp.bfloat16),
            pltpu.SemaphoreType.DMA((len(fetched),)),
        ],
    )
    return pl.pallas_call(
        functools.partial(attend_kernel, merge=merge, fetched_count=len(fetched)),
        grid_spec=spec,
        out_shape=[jax.ShapeDtypeStruct((count, n, KEY_VALUE_RANK), jnp.bfloat16) for n in heads_out]
        + [jax.ShapeDtypeStruct((count, LANES), jnp.float32)],
        compiler_params=pltpu.CompilerParams(vmem_limit_bytes=56 * 1024 * 1024),
        cost_estimate=pl.CostEstimate(
            flops=count * 400_000_000, bytes_accessed=12_000_000, transcendentals=count * 32768
        ),
        name="attend_merge" if merge else "attend_own",
    )(
        sel[first : first + count],
        lim[first : first + count],
        quarter,
        q_own,
        q_pair,
        *(earlier if merge else ()),
        *fetched,
    )


def take_kernel(asked, *refs):
    blocks, found = refs[:-1], refs[-1]
    for to in range(found.shape[0]):
        for p, block in enumerate(blocks):
            for slot in range(CAP):
                found[to, p * CAP + slot] = block[asked[p, to, slot]]


def take(asked, blocks):
    count, plane, _ = asked.shape
    tile = blocks[0].shape[1:]
    return pl.pallas_call(
        take_kernel,
        in_specs=[pl.BlockSpec(memory_space=pltpu.SMEM)] + [pl.BlockSpec(memory_space=pltpu.VMEM)] * count,
        out_specs=pl.BlockSpec(memory_space=pltpu.VMEM),
        out_shape=jax.ShapeDtypeStruct((plane, count * CAP) + tile, blocks[0].dtype),
        compiler_params=pltpu.CompilerParams(vmem_limit_bytes=16 * 1024 * 1024),
        cost_estimate=pl.CostEstimate(flops=0, bytes_accessed=count * 1_500_000, transcendentals=0),
        name="take",
    )(asked, *blocks)


def index_kernel(sel, quarter, iq, weight_t, lim, *refs):
    fetched, (index_out, keys, sems) = refs[:-3], refs[-3:]
    step = pl.program_id(0)
    part = keys.shape[1]
    _, packed, lines = lines_of(part)
    picks = sel.shape[1]
    heads = iq.shape[0] * iq.shape[2]

    @pl.when(step == 0)
    def _():
        copies, at = [], 0
        for i, ref in enumerate(fetched):
            count = ref.shape[0]
            copies.append(
                pltpu.make_async_copy(
                    ref.at[:, pl.ds(packed, lines - packed), :], keys.at[pl.ds(at, count)], sems.at[i]
                )
            )
            at += count
        for copy in copies:
            copy.start()
        for copy in copies:
            copy.wait()

    weight_lane = lax.broadcasted_iota(jnp.int32, weight_t.shape, 1)
    all_dots = []
    for i in range(GROUP):
        picked = jnp.concatenate([keys[sel[step * GROUP + i, k]] for k in range(picks)], axis=0)
        all_dots.append(
            lax.dot_general(
                iq[:, i].reshape(heads, iq.shape[3]),
                picked,
                (((1,), (1,)), ((), ())),
                preferred_element_type=jnp.float32,
            )
        )
    sums = []
    for i, dots in enumerate(all_dots):
        here = weight_lane == step * GROUP + i
        weight = jnp.sum(jnp.where(here, weight_t[...], 0.0), axis=1, keepdims=True)
        sums.append(jnp.sum(jnp.maximum(dots, 0.0) * weight, axis=0, keepdims=True))
    sums = jnp.where(lim[...] >= 0, jnp.concatenate(sums, axis=0), 0.0)
    lane = lax.broadcasted_iota(jnp.int32, (GROUP, TILE), 1)
    mine = lane // part == quarter[0]
    for k in range(picks):
        at = k * part // TILE * TILE
        turn = (quarter[0] * part - (k * part - at) + TILE) % TILE
        piece = pltpu.roll(sums[:, at : at + TILE], turn, 1)
        index_out[:, pl.ds(k * TILE, TILE)] = jnp.where(mine, piece, 0.0)


def index(sel, quarter, iq, weight_t, lim, fetched):
    queries, picks = sel.shape
    part = lim.shape[1] // picks
    slots = sum(f.shape[0] for f in fetched)
    spec = pltpu.PrefetchScalarGridSpec(
        num_scalar_prefetch=2,
        grid=(queries // GROUP,),
        in_specs=[
            pl.BlockSpec((iq.shape[0], GROUP) + iq.shape[2:], lambda i, *_: (0, i, 0, 0)),
            pl.BlockSpec(weight_t.shape, lambda i, *_: (0, 0)),
            pl.BlockSpec((GROUP, lim.shape[1]), lambda i, *_: (i, 0)),
        ]
        + [pl.BlockSpec(memory_space=pl.ANY)] * len(fetched),
        out_specs=pl.BlockSpec((GROUP, picks * TILE), lambda i, *_: (i, 0)),
        scratch_shapes=[
            pltpu.VMEM((slots, part, LANES), jnp.bfloat16),
            pltpu.SemaphoreType.DMA((len(fetched),)),
        ],
    )
    return pl.pallas_call(
        index_kernel,
        grid_spec=spec,
        out_shape=jax.ShapeDtypeStruct((queries, picks * TILE), jnp.float32),
        compiler_params=pltpu.CompilerParams(vmem_limit_bytes=16 * 1024 * 1024),
        name="index",
    )(sel, quarter, iq, weight_t, lim, *fetched)


def ring_blocks(block, axis, size):
    forward = [(i, (i + 1) % size) for i in range(size)]
    backward = [(i, (i - 1) % size) for i in range(size)]
    up = down = block
    got = {0: block}
    for d in range(1, size // 2):
        up = lax.ppermute(up, axis, forward)
        down = lax.ppermute(down, axis, backward)
        got[size - d], got[d] = up, down
    half = block.shape[0] // 2
    got[size // 2] = jnp.concatenate(
        [lax.ppermute(up[:half], axis, forward), lax.ppermute(down[half:], axis, backward)]
    )
    return got


def rounds_of(size):
    near = size // 4
    return [
        [0],
        [e for d in range(1, near + 1) for e in (d, size - d)],
        [e for d in range(near + 1, size // 2) for e in (d, size - d)] + [size // 2],
    ]


def pairings():
    near, far = (lambda y: y ^ 1), (lambda y: 3 - y)
    rows = [(4 * c + y, 4 * c + (near, far)[c](y)) for c in range(2) for y in range(4)]
    heads = [(4 * c + y, 4 * c + (far, near)[c](y)) for c in range(2) for y in range(4)]
    return rows, heads


def shards(queries, latent, index_queries, index_weights, index_keys, request_tiles, selection):
    z_count, x_count, c_count, y_count = (lax.axis_size(a) for a in ("z", "x", "c", "y"))
    z, x, c, y = (lax.axis_index(a) for a in ("z", "x", "c", "y"))
    plane = x_count * c_count
    here = x * c_count + c
    query_count, local_heads, _ = queries.shape
    index_heads = index_queries.shape[1]
    tile_count = latent.shape[0] // TILE
    part = TILE // y_count
    picks = selection.shape[1]
    _, packed, lines = lines_of(part)
    row_pairs, head_pairs = pairings()

    def quarter(a):
        return lax.dynamic_index_in_dim(a.reshape(tile_count, y_count, part, a.shape[1]), y, 1, False)

    own_rows, own_keys = quarter(latent), quarter(index_keys)
    rotary = own_rows[:, :, KEY_VALUE_RANK:]
    own = jnp.concatenate(
        [own_rows[:, :, j * LANES : (j + 1) * LANES] for j in range(COLUMNS)]
        + [jnp.concatenate([rotary[:, : part // 2], rotary[:, part // 2 :]], axis=2), own_keys],
        axis=1,
    )

    q_pair = lax.ppermute(queries, ("c", "y"), head_pairs)
    weight_rows = jnp.pad(index_weights, ((0, 0), (0, LANES - index_heads)))
    joined = jnp.concatenate([index_queries, weight_rows.reshape(-1, index_heads, LANES)], axis=0)
    joined = lax.all_gather(joined, "y")
    weights = joined[:, query_count:].reshape(y_count, query_count, LANES)[:, :, :index_heads]
    key_scale = index_keys.shape[1] ** -0.5
    weight_t = jnp.transpose(weights.astype(jnp.float32), (0, 2, 1)).reshape(-1, query_count) * key_scale

    wanted = request_tiles[0]
    plans = lax.all_gather(wanted, ("x", "c")).reshape(plane, z_count, plane, CAP)
    plans = lax.dynamic_index_in_dim(plans, here, 2, False)

    place = {}
    base = 0
    for distances in rounds_of(z_count):
        for p, d in enumerate(distances):
            place[d] = (base + p * CAP, len(distances) * CAP)
        base += plane * len(distances) * CAP
    owner = selection // CAP
    distance = (owner // plane - z) % z_count
    first = sum(jnp.where(distance == d, place[d][0], 0) for d in place)
    stride = sum(jnp.where(distance == d, place[d][1], 0) for d in place)
    rows_at = first + (owner % plane) * stride + selection % CAP

    flat_wanted = wanted.reshape(-1)
    matches = selection[:, :, None] == jnp.arange(flat_wanted.shape[0], dtype=jnp.int32)
    local_tile = jnp.sum(jnp.where(matches, flat_wanted, 0), axis=2)
    tile_start = (owner * tile_count + local_tile) * TILE
    ctx_count = z_count * plane
    context = ctx_count * tile_count * TILE
    query_pos = (
        context
        - ctx_count * query_count
        + (z * plane + here) * query_count
        + jnp.arange(query_count, dtype=jnp.int32)
    )
    lim = query_pos[:, None] - tile_start
    own_lim = (lim - y * part)[:, :, None] - jnp.arange(part, dtype=jnp.int32)
    own_lim = own_lim.reshape(query_count, picks * part)
    partner = jnp.where(c == 0, y ^ 1, 3 - y).astype(jnp.int32)

    blocks = ring_blocks(own, "z", z_count)
    own_fetched, pair_fetched = [], []
    for r, distances in enumerate(rounds_of(z_count)):
        asked = jnp.stack(
            [lax.dynamic_index_in_dim(plans, (z + d) % z_count, 1, False) for d in distances]
        )
        found = take(asked, [blocks[d] for d in distances])
        if r == 1:
            found, q_pair, own_fetched[0] = lax.optimization_barrier((found, q_pair, own_fetched[0]))
        if r == 2:
            found, joined, weight_t, own_lim, lim, rows_at = lax.optimization_barrier(
                (found, joined, weight_t, own_lim, lim, rows_at)
            )
        moved = lax.all_to_all(found.reshape(plane, -1, LANES), ("x", "c"), split_axis=0, concat_axis=0, tiled=True)
        moved = moved.reshape(-1, lines, LANES)
        own_fetched.append(moved)
        pair_fetched.append(lax.ppermute(moved[:, :packed], ("c", "y"), row_pairs))

    lim, *pair_fetched[:2] = lax.optimization_barrier((lim, *pair_fetched[:2]))
    quarter_here = jnp.reshape(y, (1,)).astype(jnp.int32)
    earlier = list(
        attend(rows_at, lim, quarter_here, queries, q_pair, own_fetched, 0, query_count)
    )
    rows_at, earlier[0] = lax.optimization_barrier((rows_at, earlier[0]))
    index_part = index(rows_at, quarter_here, joined, weight_t, own_lim, own_fetched)
    rows_at, index_part = lax.optimization_barrier((rows_at, index_part))
    index_scores = lax.psum_scatter(index_part, "y", scatter_dimension=1, tiled=True)
    split = query_count * 5 // 8
    halves = []
    for first_query, count in ((0, split), (split, query_count - split)):
        mine, other, lse = attend(
            rows_at,
            lim,
            jnp.reshape(partner, (1,)),
            queries,
            q_pair,
            pair_fetched,
            first_query,
            count,
            earlier,
        )
        if not first_query:
            rows_at, lse, index_scores = lax.optimization_barrier((rows_at, lse, index_scores))
        other = lax.ppermute(other, ("c", "y"), head_pairs)
        halves.append([mine, other, lse])
    all_lse = jnp.concatenate([lse[:, local_heads : 2 * local_heads] for _, _, lse in halves], axis=0)
    all_lse = lax.ppermute(all_lse, ("c", "y"), head_pairs)
    attended = []
    for first_query, (mine, other, lse) in zip((0, split), halves):
        lse, other_lse = lse[:, :local_heads], all_lse[first_query : first_query + lse.shape[0]]
        share = 1.0 / (1.0 + jnp.exp2(other_lse - lse))[..., None]
        other_share = 1.0 / (1.0 + jnp.exp2(lse - other_lse))[..., None]
        merged = mine.astype(jnp.float32) * share + other.astype(jnp.float32) * other_share
        attended.append(merged.astype(jnp.bfloat16))
    return jnp.concatenate(attended, axis=0), index_scores


def solution(mesh):
    ctx, head = mesh.devices.shape
    x_count, c_count = 4, 2
    grid = Mesh(
        mesh.devices.reshape(ctx // (x_count * c_count), x_count, c_count, head), ("z", "x", "c", "y")
    )
    ctx_axes = ("z", "x", "c")
    return jax.shard_map(
        shards,
        mesh=grid,
        in_specs=(
            P(ctx_axes, "y", None),
            P(ctx_axes, None),
            P(ctx_axes, "y", None),
            P(ctx_axes, "y"),
            P(ctx_axes, None),
            P(ctx_axes, None, None),
            P(ctx_axes, None),
        ),
        out_specs=(P(ctx_axes, "y", None), P(ctx_axes, "y")),
        check_vma=False,
    )
```

```python
import functools

import jax
import jax.numpy as jnp
from jax import lax
from jax.experimental import pallas as pl
from jax.experimental.pallas import tpu as pltpu
from jax.sharding import Mesh, PartitionSpec as P

KEY_VALUE_RANK = 512
LANES = 128
COLUMNS = KEY_VALUE_RANK // LANES
TILE = 128
CAP = 2
PART = 32
GROUP = 8
BATCH = 8
SCALE = 192.0 ** -0.5
LOG2_E = 1.4426950408889634
MASKED = -1e30


def lines_of(part):
    latent = COLUMNS * part
    return latent, latent + part // 2, latent + part // 2 + part


def attend_kernel(sel, lim, quarter, q_own, q_pair, *refs, merge, fetched_count, first_query):
    refs = list(refs)
    earlier, earlier_lse = (refs.pop(0), refs.pop(0)) if merge else (None, None)
    fetched, outs, (rows, sems) = refs[:fetched_count], refs[fetched_count:-2], refs[-2:]
    lse = outs[-1]
    step = pl.program_id(0)
    picks = sel.shape[1]
    half_heads = q_own.shape[1]
    heads = 2 * half_heads
    part = PART
    low = part // 2

    @pl.when(step == 0)
    def _():
        copies, at = [], 0
        for ref in fetched:
            size = ref.shape[0]
            copies.append(
                pltpu.make_async_copy(
                    ref.at[:, pl.ds(0, rows.shape[1])], rows.at[pl.ds(at, size)], sems.at[len(copies)]
                )
            )
            at += size
        for copy in copies:
            copy.start()
        for copy in copies:
            copy.wait()

    row = lax.broadcasted_iota(jnp.int32, (low, 2 * heads), 0)
    lane = lax.broadcasted_iota(jnp.int32, (low, 2 * heads), 1)
    place = jnp.where(lane < heads, row, row + low) + quarter[0] * part
    head = lax.broadcasted_iota(jnp.int32, (heads, 2 * heads), 0)
    own_lane = lax.broadcasted_iota(jnp.int32, (heads, 2 * heads), 1) == head

    def half_rows(slot, upper):
        return jnp.concatenate(
            [rows[slot, pl.ds(j * part + upper * low, low), :] for j in range(COLUMNS)], axis=1
        )

    def scores_of(i):
        query = first_query + step * GROUP + i
        here = jnp.concatenate([q_own[i], q_pair[i]], axis=0)
        value, rotary = here[:, :KEY_VALUE_RANK], here[:, KEY_VALUE_RANK:]
        no_value, no_rotary = jnp.zeros_like(value), jnp.zeros_like(rotary)
        weights = jnp.concatenate(
            [
                jnp.concatenate([value, no_value, rotary, no_rotary], axis=1),
                jnp.concatenate([no_value, value, no_rotary, rotary], axis=1),
            ],
            axis=0,
        )
        lines = []
        for k in range(picks):
            slot = sel[query, k]
            lines.append(
                jnp.concatenate(
                    [half_rows(slot, 0), half_rows(slot, 1), rows[slot, pl.ds(COLUMNS * part, low), :]], axis=1
                )
            )
        scores = lax.dot_general(
            jnp.concatenate(lines, axis=0),
            weights,
            (((1,), (1,)), ((), ())),
            preferred_element_type=jnp.float32,
        )
        scores = scores * (SCALE * LOG2_E)
        return jnp.concatenate(
            [
                jnp.where(place <= lim[query, k], scores[k * low : (k + 1) * low], MASKED)
                for k in range(picks)
            ],
            axis=0,
        )

    def both(row, op):
        return op(row, jnp.concatenate([row[:, heads:], row[:, :heads]], axis=1))

    for first in range(0, GROUP, BATCH):
        batch = range(first, first + BATCH)
        scores = [scores_of(i) for i in batch]
        probs, kept = [], []
        for i, s in zip(batch, scores):
            peak = both(jnp.max(s, axis=0, keepdims=True), jnp.maximum)
            p = jnp.exp2(s - peak)
            total = both(jnp.sum(p, axis=0, keepdims=True), jnp.add)
            level = peak + jnp.log2(total)
            if merge:
                before = earlier_lse[pl.ds(i, 1), :]
                top = jnp.maximum(before, level)
                old, new = jnp.exp2(before - top), jnp.exp2(level - top)
                share = 1.0 / (old + new)
                level = top + jnp.log2(old + new)
                kept.append(jnp.sum(jnp.where(own_lane, old * share, 0.0), axis=1, keepdims=True))
                p = p * (new * share / total)
            else:
                p = p * (1.0 / total)
            lse[pl.ds(i, 1), :] = level
            probs.append(jnp.transpose(p.astype(jnp.bfloat16)))
        for j, (i, p) in enumerate(zip(batch, probs)):
            query = first_query + step * GROUP + i
            summed = earlier[i].astype(jnp.float32) * kept[j] if merge else 0.0
            for upper in range(2):
                values = jnp.concatenate([half_rows(sel[query, k], upper) for k in range(picks)], axis=0)
                summed = summed + jnp.dot(
                    p[upper * heads : (upper + 1) * heads], values, preferred_element_type=jnp.float32
                )
            summed = summed.astype(jnp.bfloat16)
            if merge:
                outs[0][i] = summed[:half_heads]
                outs[1][i] = summed[half_heads:]
            else:
                outs[0][i] = summed


def attend(sel, lim, quarter, q_own, q_pair, fetched, first, count, earlier=None):
    _, heads, width = q_own.shape
    slots = sum(f.shape[0] for f in fetched)
    at = first // GROUP
    merge = earlier is not None
    lse_spec = pl.BlockSpec((GROUP, LANES), lambda i, *_: (i, 0))
    heads_out = [heads, heads] if merge else [2 * heads]
    before = [
        pl.BlockSpec((GROUP, 2 * heads, KEY_VALUE_RANK), lambda i, *_: (at + i, 0, 0)),
        pl.BlockSpec((GROUP, LANES), lambda i, *_: (at + i, 0)),
    ]
    spec = pltpu.PrefetchScalarGridSpec(
        num_scalar_prefetch=3,
        grid=(count // GROUP,),
        in_specs=[pl.BlockSpec((GROUP, heads, width), lambda i, *_: (at + i, 0, 0))] * 2
        + (before if merge else [])
        + [pl.BlockSpec(memory_space=pl.ANY)] * len(fetched),
        out_specs=[pl.BlockSpec((GROUP, n, KEY_VALUE_RANK), lambda i, *_: (i, 0, 0)) for n in heads_out]
        + [lse_spec],
        scratch_shapes=[
            pltpu.VMEM((slots, lines_of(PART)[1], LANES), jnp.bfloat16),
            pltpu.SemaphoreType.DMA((len(fetched),)),
        ],
    )
    return pl.pallas_call(
        functools.partial(attend_kernel, merge=merge, fetched_count=len(fetched), first_query=first),
        grid_spec=spec,
        out_shape=[jax.ShapeDtypeStruct((count, n, KEY_VALUE_RANK), jnp.bfloat16) for n in heads_out]
        + [jax.ShapeDtypeStruct((count, LANES), jnp.float32)],
        compiler_params=pltpu.CompilerParams(vmem_limit_bytes=56 * 1024 * 1024),
        cost_estimate=pl.CostEstimate(
            flops=count * 400_000_000, bytes_accessed=12_000_000, transcendentals=count * 32768
        ),
        name="attend_merge" if merge else "attend_own",
    )(
        sel,
        lim,
        quarter,
        q_own,
        q_pair,
        *(earlier if merge else ()),
        *fetched,
    )


def take_kernel(asked, *refs, halves):
    blocks, found = refs[:-1], refs[-1]
    whole = blocks[: len(blocks) - 2 * halves]
    for to in range(found.shape[0]):
        for p in range(len(whole) + halves):
            for slot in range(CAP):
                at, tile = p * CAP + slot, asked[p, to, slot]
                if p < len(whole):
                    found[to, at] = whole[p][tile]
                else:
                    low, high = blocks[-2:]
                    count = low.shape[0]
                    found[to, at] = jnp.where(
                        tile < count, low[jnp.minimum(tile, count - 1)], high[jnp.maximum(tile - count, 0)]
                    )


def take(asked, blocks):
    count, plane, _ = asked.shape
    halves = isinstance(blocks[-1], tuple)
    if halves:
        blocks = [*blocks[:-1], *blocks[-1]]
    tile = blocks[0].shape[1:]
    return pl.pallas_call(
        functools.partial(take_kernel, halves=halves),
        in_specs=[pl.BlockSpec(memory_space=pltpu.SMEM)] + [pl.BlockSpec(memory_space=pltpu.VMEM)] * len(blocks),
        out_specs=pl.BlockSpec(memory_space=pltpu.VMEM),
        out_shape=jax.ShapeDtypeStruct((plane, count * CAP) + tile, blocks[0].dtype),
        compiler_params=pltpu.CompilerParams(vmem_limit_bytes=16 * 1024 * 1024),
        cost_estimate=pl.CostEstimate(flops=0, bytes_accessed=count * 1_500_000, transcendentals=0),
        name="take",
    )(asked, *blocks)


def index_kernel(sel, quarter, iq, weight_t, lim, *refs):
    fetched, (index_out, keys, sems) = refs[:-3], refs[-3:]
    step = pl.program_id(0)
    part = keys.shape[1]
    _, packed, lines = lines_of(part)
    picks = sel.shape[1]
    heads = iq.shape[0] * iq.shape[2]

    @pl.when(step == 0)
    def _():
        copies, at = [], 0
        for i, ref in enumerate(fetched):
            count = ref.shape[0]
            copies.append(
                pltpu.make_async_copy(
                    ref.at[:, pl.ds(packed, lines - packed), :], keys.at[pl.ds(at, count)], sems.at[i]
                )
            )
            at += count
        for copy in copies:
            copy.start()
        for copy in copies:
            copy.wait()

    weight_lane = lax.broadcasted_iota(jnp.int32, weight_t.shape, 1)
    all_dots = []
    for i in range(GROUP):
        picked = jnp.concatenate([keys[sel[step * GROUP + i, k]] for k in range(picks)], axis=0)
        all_dots.append(
            lax.dot_general(
                iq[:, i].reshape(heads, iq.shape[3]),
                picked,
                (((1,), (1,)), ((), ())),
                preferred_element_type=jnp.float32,
            )
        )
    sums = []
    for i, dots in enumerate(all_dots):
        here = weight_lane == step * GROUP + i
        weight = jnp.sum(jnp.where(here, weight_t[...], 0.0), axis=1, keepdims=True)
        sums.append(jnp.sum(jnp.maximum(dots, 0.0) * weight, axis=0, keepdims=True))
    sums = jnp.where(lim[...] >= 0, jnp.concatenate(sums, axis=0), 0.0)
    lane = lax.broadcasted_iota(jnp.int32, (GROUP, TILE), 1)
    mine = lane // part == quarter[0]
    for k in range(picks):
        at = k * part // TILE * TILE
        turn = (quarter[0] * part - (k * part - at) + TILE) % TILE
        piece = pltpu.roll(sums[:, at : at + TILE], turn, 1)
        index_out[:, pl.ds(k * TILE, TILE)] = jnp.where(mine, piece, 0.0)


def index(sel, quarter, iq, weight_t, lim, fetched):
    queries, picks = sel.shape
    part = lim.shape[1] // picks
    slots = sum(f.shape[0] for f in fetched)
    spec = pltpu.PrefetchScalarGridSpec(
        num_scalar_prefetch=2,
        grid=(queries // GROUP,),
        in_specs=[
            pl.BlockSpec((iq.shape[0], GROUP) + iq.shape[2:], lambda i, *_: (0, i, 0, 0)),
            pl.BlockSpec(weight_t.shape, lambda i, *_: (0, 0)),
            pl.BlockSpec((GROUP, lim.shape[1]), lambda i, *_: (i, 0)),
        ]
        + [pl.BlockSpec(memory_space=pl.ANY)] * len(fetched),
        out_specs=pl.BlockSpec((GROUP, picks * TILE), lambda i, *_: (i, 0)),
        scratch_shapes=[
            pltpu.VMEM((slots, part, LANES), jnp.bfloat16),
            pltpu.SemaphoreType.DMA((len(fetched),)),
        ],
    )
    return pl.pallas_call(
        index_kernel,
        grid_spec=spec,
        out_shape=jax.ShapeDtypeStruct((queries, picks * TILE), jnp.float32),
        compiler_params=pltpu.CompilerParams(vmem_limit_bytes=16 * 1024 * 1024),
        name="index",
    )(sel, quarter, iq, weight_t, lim, *fetched)


def ring_blocks(block, axis, size):
    forward = [(i, (i + 1) % size) for i in range(size)]
    backward = [(i, (i - 1) % size) for i in range(size)]
    up = down = block
    got = {0: block}
    for d in range(1, size // 2):
        up = lax.ppermute(up, axis, forward)
        down = lax.ppermute(down, axis, backward)
        got[size - d], got[d] = up, down
    half = block.shape[0] // 2
    got[size // 2] = lax.ppermute(up[:half], axis, forward), lax.ppermute(down[half:], axis, backward)
    return got


def rounds_of(size):
    near = size // 4
    return [
        [0],
        [e for d in range(1, near + 1) for e in (d, size - d)],
        [e for d in range(near + 1, size // 2) for e in (d, size - d)] + [size // 2],
    ]


def pairings():
    near, far = (lambda y: y ^ 1), (lambda y: 3 - y)
    rows = [(4 * c + y, 4 * c + (near, far)[c](y)) for c in range(2) for y in range(4)]
    heads = [(4 * c + y, 4 * c + (far, near)[c](y)) for c in range(2) for y in range(4)]
    return rows, heads


def shards(queries, latent, index_queries, index_weights, index_keys, request_tiles, selection):
    z_count, x_count, c_count, y_count = (lax.axis_size(a) for a in ("z", "x", "c", "y"))
    z, x, c, y = (lax.axis_index(a) for a in ("z", "x", "c", "y"))
    plane = x_count * c_count
    here = x * c_count + c
    query_count, local_heads, _ = queries.shape
    index_heads = index_queries.shape[1]
    tile_count = latent.shape[0] // TILE
    part = TILE // y_count
    picks = selection.shape[1]
    lines = lines_of(part)[2]
    row_pairs, head_pairs = pairings()

    def quarter(a):
        return lax.dynamic_index_in_dim(a.reshape(tile_count, y_count, part, a.shape[1]), y, 1, False)

    own_rows, own_keys = quarter(latent), quarter(index_keys)
    rotary = own_rows[:, :, KEY_VALUE_RANK:]
    own = jnp.concatenate(
        [own_rows[:, :, j * LANES : (j + 1) * LANES] for j in range(COLUMNS)]
        + [jnp.concatenate([rotary[:, : part // 2], rotary[:, part // 2 :]], axis=2), own_keys],
        axis=1,
    )

    q_pair = lax.ppermute(queries, ("c", "y"), head_pairs)
    weight_rows = jnp.pad(index_weights, ((0, 0), (0, LANES - index_heads)))
    joined = jnp.concatenate([index_queries, weight_rows.reshape(-1, index_heads, LANES)], axis=0)
    joined = lax.all_gather(joined, "y")
    wanted = request_tiles[0]
    plans = lax.all_gather(wanted, ("x", "c")).reshape(plane, z_count, plane, CAP)
    plans = lax.dynamic_index_in_dim(plans, here, 2, False)

    place = {}
    base = 0
    for distances in rounds_of(z_count):
        for p, d in enumerate(distances):
            place[d] = (base + p * CAP, len(distances) * CAP)
        base += plane * len(distances) * CAP
    owner = selection // CAP
    distance = (owner // plane - z) % z_count
    first = sum(jnp.where(distance == d, place[d][0], 0) for d in place)
    stride = sum(jnp.where(distance == d, place[d][1], 0) for d in place)
    rows_at = first + (owner % plane) * stride + selection % CAP

    flat_wanted = wanted.reshape(-1)
    matches = selection[:, :, None] == jnp.arange(flat_wanted.shape[0], dtype=jnp.int32)
    local_tile = jnp.sum(jnp.where(matches, flat_wanted, 0), axis=2)
    tile_start = (owner * tile_count + local_tile) * TILE
    ctx_count = z_count * plane
    context = ctx_count * tile_count * TILE
    query_pos = (
        context
        - ctx_count * query_count
        + (z * plane + here) * query_count
        + jnp.arange(query_count, dtype=jnp.int32)
    )
    lim = query_pos[:, None] - tile_start
    own_lim = (lim - y * part)[:, :, None] - jnp.arange(part, dtype=jnp.int32)
    own_lim = own_lim.reshape(query_count, picks * part)
    partner = jnp.where(c == 0, y ^ 1, 3 - y).astype(jnp.int32)

    blocks = ring_blocks(own, "z", z_count)
    own_fetched, pair_fetched = [], []
    for r, distances in enumerate(rounds_of(z_count)):
        asked = jnp.stack(
            [lax.dynamic_index_in_dim(plans, (z + d) % z_count, 1, False) for d in distances]
        )
        found = take(asked, [blocks[d] for d in distances])
        if r == 1:
            found, q_pair, own_fetched[0] = lax.optimization_barrier((found, q_pair, own_fetched[0]))
        if r == 2:
            found, own_fetched[1], joined, own_lim, lim, rows_at = lax.optimization_barrier(
                (found, own_fetched[1], joined, own_lim, lim, rows_at)
            )
            pair_fetched.append(lax.ppermute(own_fetched[1], ("c", "y"), row_pairs))
            weights = joined[:, query_count:].reshape(y_count, query_count, LANES)[:, :, :index_heads]
            key_scale = index_keys.shape[1] ** -0.5
            weight_t = jnp.transpose(weights.astype(jnp.float32), (0, 2, 1)).reshape(-1, query_count) * key_scale
        moved = lax.all_to_all(found.reshape(plane, -1, LANES), ("x", "c"), split_axis=0, concat_axis=0, tiled=True)
        moved = moved.reshape(-1, lines, LANES)
        own_fetched.append(moved)
        if r != 1:
            pair_fetched.append(lax.ppermute(moved, ("c", "y"), row_pairs))

    lim, weight_t, pair_fetched[1] = lax.optimization_barrier((lim, weight_t, pair_fetched[1]))
    quarter_here = jnp.reshape(y, (1,)).astype(jnp.int32)
    earlier = list(
        attend(rows_at, lim, quarter_here, queries, q_pair, own_fetched, 0, query_count)
    )
    rows_at, earlier[0], pair_fetched[0] = lax.optimization_barrier((rows_at, earlier[0], pair_fetched[0]))
    index_part = index(rows_at, quarter_here, joined, weight_t, own_lim, own_fetched)
    rows_at, index_part = lax.optimization_barrier((rows_at, index_part))
    index_scores = lax.psum_scatter(index_part, "y", scatter_dimension=1, tiled=True)
    split = query_count * 3 // 4
    halves = []
    for first_query, count in ((0, split), (split, query_count - split)):
        mine, other, lse = attend(
            rows_at,
            lim,
            jnp.reshape(partner, (1,)),
            queries,
            q_pair,
            pair_fetched,
            first_query,
            count,
            earlier,
        )
        if not first_query:
            rows_at, lse, index_scores = lax.optimization_barrier((rows_at, lse, index_scores))
        other = lax.ppermute(other, ("c", "y"), head_pairs)
        halves.append([mine, other, lse])
    all_lse = jnp.concatenate([lse[:, local_heads : 2 * local_heads] for _, _, lse in halves], axis=0)
    all_lse = lax.ppermute(all_lse, ("c", "y"), head_pairs)
    attended = []
    for first_query, (mine, other, lse) in zip((0, split), halves):
        lse, other_lse = lse[:, :local_heads], all_lse[first_query : first_query + lse.shape[0]]
        share = 1.0 / (1.0 + jnp.exp2(other_lse - lse))[..., None]
        other_share = 1.0 / (1.0 + jnp.exp2(lse - other_lse))[..., None]
        merged = mine.astype(jnp.float32) * share + other.astype(jnp.float32) * other_share
        attended.append(merged.astype(jnp.bfloat16))
    return jnp.concatenate(attended, axis=0), index_scores


def solution(mesh):
    ctx, head = mesh.devices.shape
    x_count, c_count = 4, 2
    grid = Mesh(
        mesh.devices.reshape(ctx // (x_count * c_count), x_count, c_count, head), ("z", "x", "c", "y")
    )
    ctx_axes = ("z", "x", "c")
    return jax.shard_map(
        shards,
        mesh=grid,
        in_specs=(
            P(ctx_axes, "y", None),
            P(ctx_axes, None),
            P(ctx_axes, "y", None),
            P(ctx_axes, "y"),
            P(ctx_axes, None),
            P(ctx_axes, None, None),
            P(ctx_axes, None),
        ),
        out_specs=(P(ctx_axes, "y", None), P(ctx_axes, "y")),
        check_vma=False,
    )
```

```python
import functools

import jax
import jax.numpy as jnp
from jax import lax
from jax.experimental import pallas as pl
from jax.experimental.pallas import tpu as pltpu
from jax.sharding import Mesh, PartitionSpec as P

KEY_VALUE_RANK = 512
LANES = 128
COLUMNS = KEY_VALUE_RANK // LANES
TILE = 128
CAP = 2
PART = 32
GROUP = 16
BATCH = 8
SCALE = 192.0 ** -0.5
LOG2_E = 1.4426950408889634
MASKED = -1e30


def lines_of(part):
    latent = COLUMNS * part
    return latent, latent + part // 2, latent + part // 2 + part


def attend_kernel(sel, lim, quarter, q_own, q_pair, *refs, merge, fetched_count, first_query):
    refs = list(refs)
    earlier, earlier_lse = (refs.pop(0), refs.pop(0)) if merge else (None, None)
    fetched, outs, (rows, sems) = refs[:fetched_count], refs[fetched_count:-2], refs[-2:]
    lse = outs[-1]
    step = pl.program_id(0)
    picks = sel.shape[1]
    half_heads = q_own.shape[1]
    heads = 2 * half_heads
    part = PART
    low = part // 2

    @pl.when(step == 0)
    def _():
        copies, at = [], 0
        for ref in fetched:
            size = ref.shape[0]
            copies.append(
                pltpu.make_async_copy(
                    ref.at[:, pl.ds(0, rows.shape[1])], rows.at[pl.ds(at, size)], sems.at[len(copies)]
                )
            )
            at += size
        for copy in copies:
            copy.start()
        for copy in copies:
            copy.wait()

    row = lax.broadcasted_iota(jnp.int32, (low, 2 * heads), 0)
    lane = lax.broadcasted_iota(jnp.int32, (low, 2 * heads), 1)
    place = jnp.where(lane < heads, row, row + low) + quarter[0] * part
    head = lax.broadcasted_iota(jnp.int32, (heads, 2 * heads), 0)
    own_lane = lax.broadcasted_iota(jnp.int32, (heads, 2 * heads), 1) == head

    def half_rows(slot, upper):
        return jnp.concatenate(
            [rows[slot, pl.ds(j * part + upper * low, low), :] for j in range(COLUMNS)], axis=1
        )

    def scores_of(i):
        query = first_query + step * GROUP + i
        here = jnp.concatenate([q_own[i], q_pair[i]], axis=0)
        value, rotary = here[:, :KEY_VALUE_RANK], here[:, KEY_VALUE_RANK:]
        no_value, no_rotary = jnp.zeros_like(value), jnp.zeros_like(rotary)
        weights = jnp.concatenate(
            [
                jnp.concatenate([value, no_value, rotary, no_rotary], axis=1),
                jnp.concatenate([no_value, value, no_rotary, rotary], axis=1),
            ],
            axis=0,
        )
        lines = []
        for k in range(picks):
            slot = sel[query, k]
            lines.append(
                jnp.concatenate(
                    [half_rows(slot, 0), half_rows(slot, 1), rows[slot, pl.ds(COLUMNS * part, low), :]], axis=1
                )
            )
        scores = lax.dot_general(
            jnp.concatenate(lines, axis=0),
            weights,
            (((1,), (1,)), ((), ())),
            preferred_element_type=jnp.float32,
        )
        scores = scores * (SCALE * LOG2_E)
        return jnp.concatenate(
            [
                jnp.where(place <= lim[query, k], scores[k * low : (k + 1) * low], MASKED)
                for k in range(picks)
            ],
            axis=0,
        )

    def both(row, op):
        return op(row, jnp.concatenate([row[:, heads:], row[:, :heads]], axis=1))

    for first in range(0, GROUP, BATCH):
        batch = range(first, first + BATCH)
        scores = [scores_of(i) for i in batch]
        probs, kept = [], []
        for i, s in zip(batch, scores):
            peak = both(jnp.max(s, axis=0, keepdims=True), jnp.maximum)
            p = jnp.exp2(s - peak)
            total = both(jnp.sum(p, axis=0, keepdims=True), jnp.add)
            level = peak + jnp.log2(total)
            if merge:
                before = earlier_lse[pl.ds(i, 1), :]
                top = jnp.maximum(before, level)
                old, new = jnp.exp2(before - top), jnp.exp2(level - top)
                share = 1.0 / (old + new)
                level = top + jnp.log2(old + new)
                kept.append(jnp.sum(jnp.where(own_lane, old * share, 0.0), axis=1, keepdims=True))
                p = p * (new * share / total)
            else:
                p = p * (1.0 / total)
            lse[pl.ds(i, 1), :] = level
            probs.append(jnp.transpose(p.astype(jnp.bfloat16)))
        for j, (i, p) in enumerate(zip(batch, probs)):
            query = first_query + step * GROUP + i
            summed = earlier[i].astype(jnp.float32) * kept[j] if merge else 0.0
            for upper in range(2):
                values = jnp.concatenate([half_rows(sel[query, k], upper) for k in range(picks)], axis=0)
                summed = summed + jnp.dot(
                    p[upper * heads : (upper + 1) * heads], values, preferred_element_type=jnp.float32
                )
            summed = summed.astype(jnp.bfloat16)
            if merge:
                outs[0][i] = summed[:half_heads]
                outs[1][i] = summed[half_heads:]
            else:
                outs[0][i] = summed


def attend(sel, lim, quarter, q_own, q_pair, fetched, first, count, earlier=None):
    _, heads, width = q_own.shape
    slots = sum(f.shape[0] for f in fetched)
    at = first // GROUP
    merge = earlier is not None
    lse_spec = pl.BlockSpec((GROUP, LANES), lambda i, *_: (i, 0))
    heads_out = [heads, heads] if merge else [2 * heads]
    before = [
        pl.BlockSpec((GROUP, 2 * heads, KEY_VALUE_RANK), lambda i, *_: (at + i, 0, 0)),
        pl.BlockSpec((GROUP, LANES), lambda i, *_: (at + i, 0)),
    ]
    spec = pltpu.PrefetchScalarGridSpec(
        num_scalar_prefetch=3,
        grid=(count // GROUP,),
        in_specs=[pl.BlockSpec((GROUP, heads, width), lambda i, *_: (at + i, 0, 0))] * 2
        + (before if merge else [])
        + [pl.BlockSpec(memory_space=pl.ANY)] * len(fetched),
        out_specs=[pl.BlockSpec((GROUP, n, KEY_VALUE_RANK), lambda i, *_: (i, 0, 0)) for n in heads_out]
        + [lse_spec],
        scratch_shapes=[
            pltpu.VMEM((slots, lines_of(PART)[1], LANES), jnp.bfloat16),
            pltpu.SemaphoreType.DMA((len(fetched),)),
        ],
    )
    return pl.pallas_call(
        functools.partial(attend_kernel, merge=merge, fetched_count=len(fetched), first_query=first),
        grid_spec=spec,
        out_shape=[jax.ShapeDtypeStruct((count, n, KEY_VALUE_RANK), jnp.bfloat16) for n in heads_out]
        + [jax.ShapeDtypeStruct((count, LANES), jnp.float32)],
        compiler_params=pltpu.CompilerParams(vmem_limit_bytes=56 * 1024 * 1024),
        cost_estimate=pl.CostEstimate(
            flops=count * 400_000_000, bytes_accessed=12_000_000, transcendentals=count * 32768
        ),
        name="attend_merge" if merge else "attend_own",
    )(
        sel,
        lim,
        quarter,
        q_own,
        q_pair,
        *(earlier if merge else ()),
        *fetched,
    )


def take_kernel(asked, *refs, halves):
    blocks, found = refs[:-1], refs[-1]
    whole = blocks[: len(blocks) - 2 * halves]
    for to in range(found.shape[0]):
        for p in range(len(whole) + halves):
            for slot in range(CAP):
                at, tile = p * CAP + slot, asked[p, to, slot]
                if p < len(whole):
                    found[to, at] = whole[p][tile]
                else:
                    low, high = blocks[-2:]
                    count = low.shape[0]
                    found[to, at] = jnp.where(
                        tile < count, low[jnp.minimum(tile, count - 1)], high[jnp.maximum(tile - count, 0)]
                    )


def take(asked, blocks):
    count, plane, _ = asked.shape
    halves = isinstance(blocks[-1], tuple)
    if halves:
        blocks = [*blocks[:-1], *blocks[-1]]
    tile = blocks[0].shape[1:]
    return pl.pallas_call(
        functools.partial(take_kernel, halves=halves),
        in_specs=[pl.BlockSpec(memory_space=pltpu.SMEM)] + [pl.BlockSpec(memory_space=pltpu.VMEM)] * len(blocks),
        out_specs=pl.BlockSpec(memory_space=pltpu.VMEM),
        out_shape=jax.ShapeDtypeStruct((plane, count * CAP) + tile, blocks[0].dtype),
        compiler_params=pltpu.CompilerParams(vmem_limit_bytes=16 * 1024 * 1024),
        cost_estimate=pl.CostEstimate(flops=0, bytes_accessed=count * 1_500_000, transcendentals=0),
        name="take",
    )(asked, *blocks)


def index_kernel(sel, quarter, iq, weight_t, lim, *refs):
    fetched, (index_out, keys, sems) = refs[:-3], refs[-3:]
    step = pl.program_id(0)
    part = keys.shape[1]
    _, packed, lines = lines_of(part)
    picks = sel.shape[1]
    heads = iq.shape[0] * iq.shape[2]

    @pl.when(step == 0)
    def _():
        copies, at = [], 0
        for i, ref in enumerate(fetched):
            count = ref.shape[0]
            copies.append(
                pltpu.make_async_copy(
                    ref.at[:, pl.ds(packed, lines - packed), :], keys.at[pl.ds(at, count)], sems.at[i]
                )
            )
            at += count
        for copy in copies:
            copy.start()
        for copy in copies:
            copy.wait()

    weight_lane = lax.broadcasted_iota(jnp.int32, weight_t.shape, 1)
    all_dots = []
    for i in range(GROUP):
        picked = jnp.concatenate([keys[sel[step * GROUP + i, k]] for k in range(picks)], axis=0)
        all_dots.append(
            lax.dot_general(
                iq[:, i].reshape(heads, iq.shape[3]),
                picked,
                (((1,), (1,)), ((), ())),
                preferred_element_type=jnp.float32,
            )
        )
    sums = []
    for i, dots in enumerate(all_dots):
        here = weight_lane == step * GROUP + i
        weight = jnp.sum(jnp.where(here, weight_t[...], 0.0), axis=1, keepdims=True)
        sums.append(jnp.sum(jnp.maximum(dots, 0.0) * weight, axis=0, keepdims=True))
    sums = jnp.where(lim[...] >= 0, jnp.concatenate(sums, axis=0), 0.0)
    lane = lax.broadcasted_iota(jnp.int32, (GROUP, TILE), 1)
    mine = lane // part == quarter[0]
    for k in range(picks):
        at = k * part // TILE * TILE
        turn = (quarter[0] * part - (k * part - at) + TILE) % TILE
        piece = pltpu.roll(sums[:, at : at + TILE], turn, 1)
        index_out[:, pl.ds(k * TILE, TILE)] = jnp.where(mine, piece, 0.0)


def index(sel, quarter, iq, weight_t, lim, fetched):
    queries, picks = sel.shape
    part = lim.shape[1] // picks
    slots = sum(f.shape[0] for f in fetched)
    spec = pltpu.PrefetchScalarGridSpec(
        num_scalar_prefetch=2,
        grid=(queries // GROUP,),
        in_specs=[
            pl.BlockSpec((iq.shape[0], GROUP) + iq.shape[2:], lambda i, *_: (0, i, 0, 0)),
            pl.BlockSpec(weight_t.shape, lambda i, *_: (0, 0)),
            pl.BlockSpec((GROUP, lim.shape[1]), lambda i, *_: (i, 0)),
        ]
        + [pl.BlockSpec(memory_space=pl.ANY)] * len(fetched),
        out_specs=pl.BlockSpec((GROUP, picks * TILE), lambda i, *_: (i, 0)),
        scratch_shapes=[
            pltpu.VMEM((slots, part, LANES), jnp.bfloat16),
            pltpu.SemaphoreType.DMA((len(fetched),)),
        ],
    )
    return pl.pallas_call(
        index_kernel,
        grid_spec=spec,
        out_shape=jax.ShapeDtypeStruct((queries, picks * TILE), jnp.float32),
        compiler_params=pltpu.CompilerParams(vmem_limit_bytes=16 * 1024 * 1024),
        name="index",
    )(sel, quarter, iq, weight_t, lim, *fetched)


def ring_blocks(block, axis, size):
    forward = [(i, (i + 1) % size) for i in range(size)]
    backward = [(i, (i - 1) % size) for i in range(size)]
    up = down = block
    got = {0: block}
    for d in range(1, size // 2):
        up = lax.ppermute(up, axis, forward)
        down = lax.ppermute(down, axis, backward)
        got[size - d], got[d] = up, down
    half = block.shape[0] // 2
    got[size // 2] = lax.ppermute(up[:half], axis, forward), lax.ppermute(down[half:], axis, backward)
    return got


def rounds_of(size):
    near = size // 4
    return [
        [0],
        [e for d in range(1, near + 1) for e in (d, size - d)],
        [e for d in range(near + 1, size // 2) for e in (d, size - d)] + [size // 2],
    ]


def pairings():
    near, far = (lambda y: y ^ 1), (lambda y: 3 - y)
    rows = [(4 * c + y, 4 * c + (near, far)[c](y)) for c in range(2) for y in range(4)]
    heads = [(4 * c + y, 4 * c + (far, near)[c](y)) for c in range(2) for y in range(4)]
    return rows, heads


def shards(queries, latent, index_queries, index_weights, index_keys, request_tiles, selection):
    z_count, x_count, c_count, y_count = (lax.axis_size(a) for a in ("z", "x", "c", "y"))
    z, x, c, y = (lax.axis_index(a) for a in ("z", "x", "c", "y"))
    plane = x_count * c_count
    here = x * c_count + c
    query_count, local_heads, _ = queries.shape
    index_heads = index_queries.shape[1]
    tile_count = latent.shape[0] // TILE
    part = TILE // y_count
    picks = selection.shape[1]
    lines = lines_of(part)[2]
    row_pairs, head_pairs = pairings()

    def quarter(a):
        return lax.dynamic_index_in_dim(a.reshape(tile_count, y_count, part, a.shape[1]), y, 1, False)

    own_rows, own_keys = quarter(latent), quarter(index_keys)
    rotary = own_rows[:, :, KEY_VALUE_RANK:]
    own = jnp.concatenate(
        [own_rows[:, :, j * LANES : (j + 1) * LANES] for j in range(COLUMNS)]
        + [jnp.concatenate([rotary[:, : part // 2], rotary[:, part // 2 :]], axis=2), own_keys],
        axis=1,
    )

    q_pair = lax.ppermute(queries, ("c", "y"), head_pairs)
    weight_rows = jnp.pad(index_weights, ((0, 0), (0, LANES - index_heads)))
    joined = jnp.concatenate([index_queries, weight_rows.reshape(-1, index_heads, LANES)], axis=0)
    joined = lax.all_gather(joined, "y")
    wanted = request_tiles[0]
    plans = lax.all_gather(wanted, ("x", "c")).reshape(plane, z_count, plane, CAP)
    plans = lax.dynamic_index_in_dim(plans, here, 2, False)

    place = {}
    base = 0
    for distances in rounds_of(z_count):
        for p, d in enumerate(distances):
            place[d] = (base + p * CAP, len(distances) * CAP)
        base += plane * len(distances) * CAP
    owner = selection // CAP
    distance = (owner // plane - z) % z_count
    first = sum(jnp.where(distance == d, place[d][0], 0) for d in place)
    stride = sum(jnp.where(distance == d, place[d][1], 0) for d in place)
    rows_at = first + (owner % plane) * stride + selection % CAP

    flat_wanted = wanted.reshape(-1)
    matches = selection[:, :, None] == jnp.arange(flat_wanted.shape[0], dtype=jnp.int32)
    local_tile = jnp.sum(jnp.where(matches, flat_wanted, 0), axis=2)
    tile_start = (owner * tile_count + local_tile) * TILE
    ctx_count = z_count * plane
    context = ctx_count * tile_count * TILE
    query_pos = (
        context
        - ctx_count * query_count
        + (z * plane + here) * query_count
        + jnp.arange(query_count, dtype=jnp.int32)
    )
    lim = query_pos[:, None] - tile_start
    own_lim = (lim - y * part)[:, :, None] - jnp.arange(part, dtype=jnp.int32)
    own_lim = own_lim.reshape(query_count, picks * part)
    partner = jnp.where(c == 0, y ^ 1, 3 - y).astype(jnp.int32)

    blocks = ring_blocks(own, "z", z_count)
    own_fetched, pair_fetched = [], []
    for r, distances in enumerate(rounds_of(z_count)):
        asked = jnp.stack(
            [lax.dynamic_index_in_dim(plans, (z + d) % z_count, 1, False) for d in distances]
        )
        found = take(asked, [blocks[d] for d in distances])
        if r == 1:
            found, q_pair, own_fetched[0] = lax.optimization_barrier((found, q_pair, own_fetched[0]))
        if r == 2:
            found, own_fetched[1], joined, own_lim, lim, rows_at = lax.optimization_barrier(
                (found, own_fetched[1], joined, own_lim, lim, rows_at)
            )
            pair_fetched.append(lax.ppermute(own_fetched[1], ("c", "y"), row_pairs))
            weights = joined[:, query_count:].reshape(y_count, query_count, LANES)[:, :, :index_heads]
            key_scale = index_keys.shape[1] ** -0.5
            weight_t = jnp.transpose(weights.astype(jnp.float32), (0, 2, 1)).reshape(-1, query_count) * key_scale
        moved = lax.all_to_all(found.reshape(plane, -1, LANES), ("x", "c"), split_axis=0, concat_axis=0, tiled=True)
        moved = moved.reshape(-1, lines, LANES)
        own_fetched.append(moved)
        if r != 1:
            pair_fetched.append(lax.ppermute(moved, ("c", "y"), row_pairs))

    lim, weight_t, pair_fetched[1] = lax.optimization_barrier((lim, weight_t, pair_fetched[1]))
    quarter_here = jnp.reshape(y, (1,)).astype(jnp.int32)
    earlier = list(
        attend(rows_at, lim, quarter_here, queries, q_pair, own_fetched, 0, query_count)
    )
    rows_at, earlier[0], pair_fetched[0] = lax.optimization_barrier((rows_at, earlier[0], pair_fetched[0]))
    index_part = index(rows_at, quarter_here, joined, weight_t, own_lim, own_fetched)
    rows_at, index_part = lax.optimization_barrier((rows_at, index_part))
    index_scores = lax.psum_scatter(index_part, "y", scatter_dimension=1, tiled=True)
    split = query_count * 3 // 4
    halves = []
    for first_query, count in ((0, split), (split, query_count - split)):
        mine, other, lse = attend(
            rows_at,
            lim,
            jnp.reshape(partner, (1,)),
            queries,
            q_pair,
            pair_fetched,
            first_query,
            count,
            earlier,
        )
        if not first_query:
            rows_at, lse, index_scores = lax.optimization_barrier((rows_at, lse, index_scores))
        other = lax.ppermute(other, ("c", "y"), head_pairs)
        halves.append([mine, other, lse])
    all_lse = jnp.concatenate([lse[:, local_heads : 2 * local_heads] for _, _, lse in halves], axis=0)
    all_lse = lax.ppermute(all_lse, ("c", "y"), head_pairs)
    attended = []
    for first_query, (mine, other, lse) in zip((0, split), halves):
        lse, other_lse = lse[:, :local_heads], all_lse[first_query : first_query + lse.shape[0]]
        share = 1.0 / (1.0 + jnp.exp2(other_lse - lse))[..., None]
        other_share = 1.0 / (1.0 + jnp.exp2(lse - other_lse))[..., None]
        merged = mine.astype(jnp.float32) * share + other.astype(jnp.float32) * other_share
        attended.append(merged.astype(jnp.bfloat16))
    return jnp.concatenate(attended, axis=0), index_scores


def solution(mesh):
    ctx, head = mesh.devices.shape
    x_count, c_count = 4, 2
    grid = Mesh(
        mesh.devices.reshape(ctx // (x_count * c_count), x_count, c_count, head), ("z", "x", "c", "y")
    )
    ctx_axes = ("z", "x", "c")
    return jax.shard_map(
        shards,
        mesh=grid,
        in_specs=(
            P(ctx_axes, "y", None),
            P(ctx_axes, None),
            P(ctx_axes, "y", None),
            P(ctx_axes, "y"),
            P(ctx_axes, None),
            P(ctx_axes, None, None),
            P(ctx_axes, None),
        ),
        out_specs=(P(ctx_axes, "y", None), P(ctx_axes, "y")),
        check_vma=False,
    )
```

```python
import functools

import jax
import jax.numpy as jnp
from jax import lax
from jax.experimental import pallas as pl
from jax.experimental.pallas import tpu as pltpu
from jax.sharding import Mesh, PartitionSpec as P

KEY_VALUE_RANK = 512
LANES = 128
COLUMNS = KEY_VALUE_RANK // LANES
TILE = 128
CAP = 2
PART = 32
GROUP = 16
BATCH = 16
SCALE = 192.0 ** -0.5
LOG2_E = 1.4426950408889634
MASKED = -1e30


def lines_of(part):
    latent = COLUMNS * part
    return latent, latent + part // 2, latent + part // 2 + part


def attend_kernel(sel, lim, quarter, q_own, q_pair, *refs, merge, fetched_count, first_query):
    refs = list(refs)
    earlier, earlier_lse = (refs.pop(0), refs.pop(0)) if merge else (None, None)
    fetched, outs, (rows, sems) = refs[:fetched_count], refs[fetched_count:-2], refs[-2:]
    lse = outs[-1]
    step = pl.program_id(0)
    picks = sel.shape[1]
    half_heads = q_own.shape[1]
    heads = 2 * half_heads
    part = PART
    low = part // 2

    @pl.when(step == 0)
    def _():
        copies, at = [], 0
        for ref in fetched:
            size = ref.shape[0]
            copies.append(
                pltpu.make_async_copy(
                    ref.at[:, pl.ds(0, rows.shape[1])], rows.at[pl.ds(at, size)], sems.at[len(copies)]
                )
            )
            at += size
        for copy in copies:
            copy.start()
        for copy in copies:
            copy.wait()

    row = lax.broadcasted_iota(jnp.int32, (low, 2 * heads), 0)
    lane = lax.broadcasted_iota(jnp.int32, (low, 2 * heads), 1)
    place = jnp.where(lane < heads, row, row + low) + quarter[0] * part
    head = lax.broadcasted_iota(jnp.int32, (heads, 2 * heads), 0)
    own_lane = lax.broadcasted_iota(jnp.int32, (heads, 2 * heads), 1) == head

    def half_rows(slot, upper):
        return jnp.concatenate(
            [rows[slot, pl.ds(j * part + upper * low, low), :] for j in range(COLUMNS)], axis=1
        )

    def scores_of(i):
        query = first_query + step * GROUP + i
        here = jnp.concatenate([q_own[i], q_pair[i]], axis=0)
        value, rotary = here[:, :KEY_VALUE_RANK], here[:, KEY_VALUE_RANK:]
        no_value, no_rotary = jnp.zeros_like(value), jnp.zeros_like(rotary)
        weights = jnp.concatenate(
            [
                jnp.concatenate([value, no_value, rotary, no_rotary], axis=1),
                jnp.concatenate([no_value, value, no_rotary, rotary], axis=1),
            ],
            axis=0,
        )
        lines = []
        for k in range(picks):
            slot = sel[query, k]
            lines.append(
                jnp.concatenate(
                    [half_rows(slot, 0), half_rows(slot, 1), rows[slot, pl.ds(COLUMNS * part, low), :]], axis=1
                )
            )
        scores = lax.dot_general(
            jnp.concatenate(lines, axis=0),
            weights,
            (((1,), (1,)), ((), ())),
            preferred_element_type=jnp.float32,
        )
        scores = scores * (SCALE * LOG2_E)
        return jnp.concatenate(
            [
                jnp.where(place <= lim[query, k], scores[k * low : (k + 1) * low], MASKED)
                for k in range(picks)
            ],
            axis=0,
        )

    def both(row, op):
        return op(row, jnp.concatenate([row[:, heads:], row[:, :heads]], axis=1))

    for first in range(0, GROUP, BATCH):
        batch = range(first, first + BATCH)
        scores = [scores_of(i) for i in batch]
        probs, kept = [], []
        for i, s in zip(batch, scores):
            peak = both(jnp.max(s, axis=0, keepdims=True), jnp.maximum)
            p = jnp.exp2(s - peak)
            total = both(jnp.sum(p, axis=0, keepdims=True), jnp.add)
            level = peak + jnp.log2(total)
            if merge:
                before = earlier_lse[pl.ds(i, 1), :]
                top = jnp.maximum(before, level)
                old, new = jnp.exp2(before - top), jnp.exp2(level - top)
                share = 1.0 / (old + new)
                level = top + jnp.log2(old + new)
                kept.append(jnp.sum(jnp.where(own_lane, old * share, 0.0), axis=1, keepdims=True))
                p = p * (new * share / total)
            else:
                p = p * (1.0 / total)
            lse[pl.ds(i, 1), :] = level
            probs.append(jnp.transpose(p.astype(jnp.bfloat16)))
        for j, (i, p) in enumerate(zip(batch, probs)):
            query = first_query + step * GROUP + i
            summed = earlier[i].astype(jnp.float32) * kept[j] if merge else 0.0
            for upper in range(2):
                values = jnp.concatenate([half_rows(sel[query, k], upper) for k in range(picks)], axis=0)
                summed = summed + jnp.dot(
                    p[upper * heads : (upper + 1) * heads], values, preferred_element_type=jnp.float32
                )
            summed = summed.astype(jnp.bfloat16)
            if merge:
                outs[0][i] = summed[:half_heads]
                outs[1][i] = summed[half_heads:]
            else:
                outs[0][i] = summed


def attend(sel, lim, quarter, q_own, q_pair, fetched, first, count, earlier=None):
    _, heads, width = q_own.shape
    slots = sum(f.shape[0] for f in fetched)
    at = first // GROUP
    merge = earlier is not None
    lse_spec = pl.BlockSpec((GROUP, LANES), lambda i, *_: (i, 0))
    heads_out = [heads, heads] if merge else [2 * heads]
    before = [
        pl.BlockSpec((GROUP, 2 * heads, KEY_VALUE_RANK), lambda i, *_: (at + i, 0, 0)),
        pl.BlockSpec((GROUP, LANES), lambda i, *_: (at + i, 0)),
    ]
    spec = pltpu.PrefetchScalarGridSpec(
        num_scalar_prefetch=3,
        grid=(count // GROUP,),
        in_specs=[pl.BlockSpec((GROUP, heads, width), lambda i, *_: (at + i, 0, 0))] * 2
        + (before if merge else [])
        + [pl.BlockSpec(memory_space=pl.ANY)] * len(fetched),
        out_specs=[pl.BlockSpec((GROUP, n, KEY_VALUE_RANK), lambda i, *_: (i, 0, 0)) for n in heads_out]
        + [lse_spec],
        scratch_shapes=[
            pltpu.VMEM((slots, lines_of(PART)[1], LANES), jnp.bfloat16),
            pltpu.SemaphoreType.DMA((len(fetched),)),
        ],
    )
    return pl.pallas_call(
        functools.partial(attend_kernel, merge=merge, fetched_count=len(fetched), first_query=first),
        grid_spec=spec,
        out_shape=[jax.ShapeDtypeStruct((count, n, KEY_VALUE_RANK), jnp.bfloat16) for n in heads_out]
        + [jax.ShapeDtypeStruct((count, LANES), jnp.float32)],
        compiler_params=pltpu.CompilerParams(vmem_limit_bytes=56 * 1024 * 1024),
        cost_estimate=pl.CostEstimate(
            flops=count * 400_000_000, bytes_accessed=12_000_000, transcendentals=count * 32768
        ),
        name="attend_merge" if merge else "attend_own",
    )(
        sel,
        lim,
        quarter,
        q_own,
        q_pair,
        *(earlier if merge else ()),
        *fetched,
    )


def take_kernel(asked, *refs, halves):
    blocks, found = refs[:-1], refs[-1]
    whole = blocks[: len(blocks) - 2 * halves]
    for to in range(found.shape[0]):
        for p in range(len(whole) + halves):
            for slot in range(CAP):
                at, tile = p * CAP + slot, asked[p, to, slot]
                if p < len(whole):
                    found[to, at] = whole[p][tile]
                else:
                    low, high = blocks[-2:]
                    count = low.shape[0]
                    found[to, at] = jnp.where(
                        tile < count, low[jnp.minimum(tile, count - 1)], high[jnp.maximum(tile - count, 0)]
                    )


def take(asked, blocks):
    count, plane, _ = asked.shape
    halves = isinstance(blocks[-1], tuple)
    if halves:
        blocks = [*blocks[:-1], *blocks[-1]]
    tile = blocks[0].shape[1:]
    return pl.pallas_call(
        functools.partial(take_kernel, halves=halves),
        in_specs=[pl.BlockSpec(memory_space=pltpu.SMEM)] + [pl.BlockSpec(memory_space=pltpu.VMEM)] * len(blocks),
        out_specs=pl.BlockSpec(memory_space=pltpu.VMEM),
        out_shape=jax.ShapeDtypeStruct((plane, count * CAP) + tile, blocks[0].dtype),
        compiler_params=pltpu.CompilerParams(vmem_limit_bytes=16 * 1024 * 1024),
        cost_estimate=pl.CostEstimate(flops=0, bytes_accessed=count * 1_500_000, transcendentals=0),
        name="take",
    )(asked, *blocks)


def index_kernel(sel, quarter, iq, weight_t, lim, *refs):
    fetched, (index_out, keys, sems) = refs[:-3], refs[-3:]
    step = pl.program_id(0)
    part = keys.shape[1]
    _, packed, lines = lines_of(part)
    picks = sel.shape[1]
    heads = iq.shape[0] * iq.shape[2]

    @pl.when(step == 0)
    def _():
        copies, at = [], 0
        for i, ref in enumerate(fetched):
            count = ref.shape[0]
            copies.append(
                pltpu.make_async_copy(
                    ref.at[:, pl.ds(packed, lines - packed), :], keys.at[pl.ds(at, count)], sems.at[i]
                )
            )
            at += count
        for copy in copies:
            copy.start()
        for copy in copies:
            copy.wait()

    weight_lane = lax.broadcasted_iota(jnp.int32, weight_t.shape, 1)
    all_dots = []
    for i in range(GROUP):
        picked = jnp.concatenate([keys[sel[step * GROUP + i, k]] for k in range(picks)], axis=0)
        all_dots.append(
            lax.dot_general(
                iq[:, i].reshape(heads, iq.shape[3]),
                picked,
                (((1,), (1,)), ((), ())),
                preferred_element_type=jnp.float32,
            )
        )
    sums = []
    for i, dots in enumerate(all_dots):
        here = weight_lane == step * GROUP + i
        weight = jnp.sum(jnp.where(here, weight_t[...], 0.0), axis=1, keepdims=True)
        sums.append(jnp.sum(jnp.maximum(dots, 0.0) * weight, axis=0, keepdims=True))
    sums = jnp.where(lim[...] >= 0, jnp.concatenate(sums, axis=0), 0.0)
    lane = lax.broadcasted_iota(jnp.int32, (GROUP, TILE), 1)
    mine = lane // part == quarter[0]
    for k in range(picks):
        at = k * part // TILE * TILE
        turn = (quarter[0] * part - (k * part - at) + TILE) % TILE
        piece = pltpu.roll(sums[:, at : at + TILE], turn, 1)
        index_out[:, pl.ds(k * TILE, TILE)] = jnp.where(mine, piece, 0.0)


def index(sel, quarter, iq, weight_t, lim, fetched):
    queries, picks = sel.shape
    part = lim.shape[1] // picks
    slots = sum(f.shape[0] for f in fetched)
    spec = pltpu.PrefetchScalarGridSpec(
        num_scalar_prefetch=2,
        grid=(queries // GROUP,),
        in_specs=[
            pl.BlockSpec((iq.shape[0], GROUP) + iq.shape[2:], lambda i, *_: (0, i, 0, 0)),
            pl.BlockSpec(weight_t.shape, lambda i, *_: (0, 0)),
            pl.BlockSpec((GROUP, lim.shape[1]), lambda i, *_: (i, 0)),
        ]
        + [pl.BlockSpec(memory_space=pl.ANY)] * len(fetched),
        out_specs=pl.BlockSpec((GROUP, picks * TILE), lambda i, *_: (i, 0)),
        scratch_shapes=[
            pltpu.VMEM((slots, part, LANES), jnp.bfloat16),
            pltpu.SemaphoreType.DMA((len(fetched),)),
        ],
    )
    return pl.pallas_call(
        index_kernel,
        grid_spec=spec,
        out_shape=jax.ShapeDtypeStruct((queries, picks * TILE), jnp.float32),
        compiler_params=pltpu.CompilerParams(vmem_limit_bytes=16 * 1024 * 1024),
        name="index",
    )(sel, quarter, iq, weight_t, lim, *fetched)


def ring_blocks(block, axis, size):
    forward = [(i, (i + 1) % size) for i in range(size)]
    backward = [(i, (i - 1) % size) for i in range(size)]
    up = down = block
    got = {0: block}
    for d in range(1, size // 2):
        up = lax.ppermute(up, axis, forward)
        down = lax.ppermute(down, axis, backward)
        got[size - d], got[d] = up, down
    half = block.shape[0] // 2
    got[size // 2] = lax.ppermute(up[:half], axis, forward), lax.ppermute(down[half:], axis, backward)
    return got


def rounds_of(size):
    near = size // 4
    return [
        [0],
        [e for d in range(1, near + 1) for e in (d, size - d)],
        [e for d in range(near + 1, size // 2) for e in (d, size - d)] + [size // 2],
    ]


def pairings():
    near, far = (lambda y: y ^ 1), (lambda y: 3 - y)
    rows = [(4 * c + y, 4 * c + (near, far)[c](y)) for c in range(2) for y in range(4)]
    heads = [(4 * c + y, 4 * c + (far, near)[c](y)) for c in range(2) for y in range(4)]
    return rows, heads


def shards(queries, latent, index_queries, index_weights, index_keys, request_tiles, selection):
    z_count, x_count, c_count, y_count = (lax.axis_size(a) for a in ("z", "x", "c", "y"))
    z, x, c, y = (lax.axis_index(a) for a in ("z", "x", "c", "y"))
    plane = x_count * c_count
    here = x * c_count + c
    query_count, local_heads, _ = queries.shape
    index_heads = index_queries.shape[1]
    tile_count = latent.shape[0] // TILE
    part = TILE // y_count
    picks = selection.shape[1]
    lines = lines_of(part)[2]
    row_pairs, head_pairs = pairings()

    def quarter(a):
        return lax.dynamic_index_in_dim(a.reshape(tile_count, y_count, part, a.shape[1]), y, 1, False)

    own_rows, own_keys = quarter(latent), quarter(index_keys)
    rotary = own_rows[:, :, KEY_VALUE_RANK:]
    own = jnp.concatenate(
        [own_rows[:, :, j * LANES : (j + 1) * LANES] for j in range(COLUMNS)]
        + [jnp.concatenate([rotary[:, : part // 2], rotary[:, part // 2 :]], axis=2), own_keys],
        axis=1,
    )

    q_pair = lax.ppermute(queries, ("c", "y"), head_pairs)
    weight_rows = jnp.pad(index_weights, ((0, 0), (0, LANES - index_heads)))
    joined = jnp.concatenate([index_queries, weight_rows.reshape(-1, index_heads, LANES)], axis=0)
    joined = lax.all_gather(joined, "y")
    wanted = request_tiles[0]
    plans = lax.all_gather(wanted, ("x", "c")).reshape(plane, z_count, plane, CAP)
    plans = lax.dynamic_index_in_dim(plans, here, 2, False)

    place = {}
    base = 0
    for distances in rounds_of(z_count):
        for p, d in enumerate(distances):
            place[d] = (base + p * CAP, len(distances) * CAP)
        base += plane * len(distances) * CAP
    owner = selection // CAP
    distance = (owner // plane - z) % z_count
    first = sum(jnp.where(distance == d, place[d][0], 0) for d in place)
    stride = sum(jnp.where(distance == d, place[d][1], 0) for d in place)
    rows_at = first + (owner % plane) * stride + selection % CAP

    flat_wanted = wanted.reshape(-1)
    matches = selection[:, :, None] == jnp.arange(flat_wanted.shape[0], dtype=jnp.int32)
    local_tile = jnp.sum(jnp.where(matches, flat_wanted, 0), axis=2)
    tile_start = (owner * tile_count + local_tile) * TILE
    ctx_count = z_count * plane
    context = ctx_count * tile_count * TILE
    query_pos = (
        context
        - ctx_count * query_count
        + (z * plane + here) * query_count
        + jnp.arange(query_count, dtype=jnp.int32)
    )
    lim = query_pos[:, None] - tile_start
    own_lim = (lim - y * part)[:, :, None] - jnp.arange(part, dtype=jnp.int32)
    own_lim = own_lim.reshape(query_count, picks * part)
    partner = jnp.where(c == 0, y ^ 1, 3 - y).astype(jnp.int32)

    blocks = ring_blocks(own, "z", z_count)
    own_fetched, pair_fetched = [], []
    for r, distances in enumerate(rounds_of(z_count)):
        asked = jnp.stack(
            [lax.dynamic_index_in_dim(plans, (z + d) % z_count, 1, False) for d in distances]
        )
        found = take(asked, [blocks[d] for d in distances])
        if r == 1:
            found, q_pair, own_fetched[0] = lax.optimization_barrier((found, q_pair, own_fetched[0]))
        if r == 2:
            found, own_fetched[1], joined, own_lim, lim, rows_at = lax.optimization_barrier(
                (found, own_fetched[1], joined, own_lim, lim, rows_at)
            )
            pair_fetched.append(lax.ppermute(own_fetched[1], ("c", "y"), row_pairs))
            weights = joined[:, query_count:].reshape(y_count, query_count, LANES)[:, :, :index_heads]
            key_scale = index_keys.shape[1] ** -0.5
            weight_t = jnp.transpose(weights.astype(jnp.float32), (0, 2, 1)).reshape(-1, query_count) * key_scale
        moved = lax.all_to_all(found.reshape(plane, -1, LANES), ("x", "c"), split_axis=0, concat_axis=0, tiled=True)
        moved = moved.reshape(-1, lines, LANES)
        own_fetched.append(moved)
        if r != 1:
            pair_fetched.append(lax.ppermute(moved, ("c", "y"), row_pairs))

    lim, weight_t, pair_fetched[1] = lax.optimization_barrier((lim, weight_t, pair_fetched[1]))
    quarter_here = jnp.reshape(y, (1,)).astype(jnp.int32)
    earlier = list(
        attend(rows_at, lim, quarter_here, queries, q_pair, own_fetched, 0, query_count)
    )
    rows_at, earlier[0], pair_fetched[0] = lax.optimization_barrier((rows_at, earlier[0], pair_fetched[0]))
    index_part = index(rows_at, quarter_here, joined, weight_t, own_lim, own_fetched)
    rows_at, index_part = lax.optimization_barrier((rows_at, index_part))
    index_scores = lax.psum_scatter(index_part, "y", scatter_dimension=1, tiled=True)
    split = query_count * 3 // 4
    halves = []
    for first_query, count in ((0, split), (split, query_count - split)):
        mine, other, lse = attend(
            rows_at,
            lim,
            jnp.reshape(partner, (1,)),
            queries,
            q_pair,
            pair_fetched,
            first_query,
            count,
            earlier,
        )
        if not first_query:
            rows_at, lse, index_scores = lax.optimization_barrier((rows_at, lse, index_scores))
        other = lax.ppermute(other, ("c", "y"), head_pairs)
        halves.append([mine, other, lse])
    all_lse = jnp.concatenate([lse[:, local_heads : 2 * local_heads] for _, _, lse in halves], axis=0)
    all_lse = lax.ppermute(all_lse, ("c", "y"), head_pairs)
    attended = []
    for first_query, (mine, other, lse) in zip((0, split), halves):
        lse, other_lse = lse[:, :local_heads], all_lse[first_query : first_query + lse.shape[0]]
        share = 1.0 / (1.0 + jnp.exp2(other_lse - lse))[..., None]
        other_share = 1.0 / (1.0 + jnp.exp2(lse - other_lse))[..., None]
        merged = mine.astype(jnp.float32) * share + other.astype(jnp.float32) * other_share
        attended.append(merged.astype(jnp.bfloat16))
    return jnp.concatenate(attended, axis=0), index_scores


def solution(mesh):
    ctx, head = mesh.devices.shape
    x_count, c_count = 4, 2
    grid = Mesh(
        mesh.devices.reshape(ctx // (x_count * c_count), x_count, c_count, head), ("z", "x", "c", "y")
    )
    ctx_axes = ("z", "x", "c")
    return jax.shard_map(
        shards,
        mesh=grid,
        in_specs=(
            P(ctx_axes, "y", None),
            P(ctx_axes, None),
            P(ctx_axes, "y", None),
            P(ctx_axes, "y"),
            P(ctx_axes, None),
            P(ctx_axes, None, None),
            P(ctx_axes, None),
        ),
        out_specs=(P(ctx_axes, "y", None), P(ctx_axes, "y")),
        check_vma=False,
    )
```
